512 devices in a mesh: chan: 128 (over x, y_hi, z, core), tblk: 4 (over y_lo).
Axes of the slice: x: 4, y: 8 (y_hi: 2, y_lo: 4; y = y_hi * 4 + y_lo), z: 8, core: 2. Of those that a mesh axis runs over, the one named last changes fastest.
Arguments:
- voltages: bfloat16 [2, 16, 2048, 1024], P(None, 'tblk', 'chan'), may hold values from -6 to 6
- calibrated_gain: float32 [2, 2048, 1024], P(None, 'chan'), may hold values from -4 to 4
- cells: int32 [2, 2048], replicated, may hold values from 0 to 126
- offsets: int32 [2, 2048], replicated, may hold values from 0 to 7
Outputs:
- images: float32 [1024, 128, 128], P(('chan', 'tblk'))
The draws below stay inside these ranges and needn't reach their ends.
Inputs may be any that keep to these rules, and one draw needn't show every extreme that they name: Each antenna's 2 x 2 footprint of cells lies on the grid.
All inputs are finite; a program needn't handle non-finite values.
Results may differ from the reference program's by a relative error of at most 0.0056.
Values may be sent and summed in bfloat16 or wider, within the bound.
No kernel may reach another device: no remote copies, remote signals or barrier semaphores. Data moves between devices by JAX's collectives and lax.ppermute only.
A program may use at most 128 MiB of HBM per device.

```python
import math
import jax
import jax.numpy as jnp
from jax import lax

ANTENNA_COUNT = 2048
CHANNEL_COUNT = 1024
GRID_CELLS = 128
TAPS = 4
FRAME_COUNT = 16


def set_ends(result, rng, low, high):
    index_at = [jax.random.randint(jax.random.fold_in(rng, axis), (), 0, length) for axis, length in enumerate(result.shape)]
    widest = result.shape.index(max(result.shape))
    neighbour = index_at[:widest] + [(index_at[widest] + 1) % result.shape[widest]] + index_at[widest + 1:]
    return result.at[tuple(index_at)].set(low).at[tuple(neighbour)].set(high)


def level_of(rng, shape, cuts, smallest, high):
    factor_of, own = 1.0, jax.random.fold_in(rng, 6)
    for position, shards_of in cuts:
        heights = jnp.exp(jax.random.uniform(jax.random.fold_in(own, position), (shards_of,), jnp.float32, smallest / len(cuts), high / len(cuts)))
        factor_of = factor_of * jnp.repeat(heights, shape[position] // shards_of).reshape([-1 if axis == position else 1 for axis in range(len(shape))])
    return factor_of


def centred(stream_key, extent, deviation, most, cuts=(), kind=jnp.bfloat16):
    values = jax.random.normal(stream_key, extent, jnp.float32) * deviation
    if len(cuts) > 0:
        values = level_of(stream_key, extent, cuts, -0.22, 0.18) * values
    return jnp.clip(values, min=-most, max=most).astype(kind)


def setup_inputs(seed: int = 0) -> dict:
    splits = jax.random.split(jax.random.key(seed), 5)
    return {
        "voltages": centred(splits[0], (2, FRAME_COUNT, ANTENNA_COUNT, CHANNEL_COUNT), 1.0, 6.0, ((1, 4), (2, 128))),
        "calibrated_gain": centred(splits[1], (2, ANTENNA_COUNT, CHANNEL_COUNT), 0.7, 4.0, ((1, 128),), jnp.float32),
        "cells": set_ends(jax.random.randint(splits[2], (2, ANTENNA_COUNT), 0, GRID_CELLS - 1), jax.random.fold_in(splits[2], 1), 0, (GRID_CELLS - 1) - 1).astype(jnp.int32),
        "offsets": set_ends(jax.random.randint(splits[3], (2, ANTENNA_COUNT), 0, 8), jax.random.fold_in(splits[3], 1), 0, 7).astype(jnp.int32),
    }


def dft_table(length):
    points = jnp.arange(length, dtype=jnp.int32)
    product = (points[:, None] * points[None, :]) % length
    phases = product.astype(jnp.float32) * (2.0 * math.pi / length)
    cosine = jnp.cos(phases)
    sines = jnp.sin(phases)
    real_rows = jnp.stack([cosine, -sines], axis=1)
    imag_rows = jnp.stack([sines, cosine], axis=1)
    return jnp.stack([real_rows, imag_rows], axis=0).astype(jnp.bfloat16)


def prototype(tap_count, channels):
    span_total = tap_count * channels
    places = jnp.arange(span_total, dtype=jnp.int32).astype(jnp.float32) + 0.5
    time_window = 0.54 - 0.46 * jnp.cos(places * (2.0 * math.pi / span_total))
    return (jnp.sinc((places - 0.5 * span_total) / channels) * time_window).reshape(tap_count, channels)


def twiddle(first_len, second, channels):
    row_points = jnp.arange(first_len, dtype=jnp.int32)
    column_positions = jnp.arange(second, dtype=jnp.int32)
    phases = ((row_points[:, None] * column_positions[None, :]) % channels).astype(jnp.float32) * (2.0 * math.pi / channels)
    return jnp.cos(phases), -jnp.sin(phases)


def channelize(extended, gains, frames):
    tap_count = extended.shape[1] - frames + 1
    antennas = extended.shape[2]
    channels = extended.shape[3]
    second = channels // 32
    filter_taps = prototype(tap_count, channels)
    summed = jnp.zeros((2, frames, antennas, channels), jnp.float32)
    for tap_index in range(tap_count):
        summed = summed + filter_taps[tap_index] * extended[:, tap_index:tap_index + frames].astype(jnp.float32)
    windowed = summed.astype(jnp.bfloat16).reshape(2, frames, antennas, 32, second)
    partial_value = jnp.einsum("cfajn,cjdk->dfakn", windowed.astype(jnp.float32), dft_table(32).astype(jnp.float32), precision=lax.Precision.HIGHEST)
    twist_real, twiddle_imaginary = twiddle(32, second, channels)
    rotated = jnp.stack([partial_value[0] * twist_real - partial_value[1] * twiddle_imaginary, partial_value[0] * twiddle_imaginary + partial_value[1] * twist_real]).astype(jnp.bfloat16)
    spectra = jnp.einsum("cfakn,cnem->aefmk", rotated.astype(jnp.float32), dft_table(second).astype(jnp.float32), precision=lax.Precision.HIGHEST)
    spectra = spectra.reshape(antennas, 2, frames, channels)
    gain_real = gains[0][:, None, :]
    gain_imag = gains[1][:, None, :]
    voltage_out = jnp.stack([spectra[:, 0] * gain_real - spectra[:, 1] * gain_imag, spectra[:, 0] * gain_imag + spectra[:, 1] * gain_real], axis=1)
    return voltage_out.astype(jnp.bfloat16)


def footprint(cells, offsets, grid_size):
    fraction = (offsets.astype(jnp.float32) + 0.5) / 8.0
    row_weight = jnp.stack([1.0 - fraction[0], fraction[0]])
    col_weight = jnp.stack([1.0 - fraction[1], fraction[1]])
    weights = row_weight[:, None, :] * col_weight[None, :, :]
    shifts = jnp.arange(2, dtype=jnp.int32)
    cell_index = (cells[0][None, None, :] + shifts[:, None, None]) * grid_size + cells[1][None, None, :] + shifts[None, :, None]
    target = jnp.stack([cell_index, cell_index + grid_size * grid_size], axis=-1)
    return weights, target


def power_block(volt_block, weights, target, grid_size, dft_grid):
    columns = volt_block.shape[-1]
    spread = weights[:, :, :, None, None] * volt_block[None, None].astype(jnp.float32)
    aperture = jax.ops.segment_sum(spread.reshape(-1, columns), target.reshape(-1), num_segments=2 * grid_size * grid_size)
    aperture = aperture.astype(jnp.bfloat16).reshape(2 * grid_size, grid_size * columns)
    matrix = dft_grid.transpose(2, 3, 0, 1).reshape(2 * grid_size, 2 * grid_size)
    halfway = jnp.dot(matrix, aperture, preferred_element_type=jnp.float32).astype(jnp.bfloat16)
    halfway = halfway.reshape(2, grid_size, grid_size, columns)
    sky_field = jnp.einsum("dkvb,dveh->ekhb", halfway.astype(jnp.float32), dft_grid.astype(jnp.float32), precision=lax.Precision.HIGHEST)
    return sky_field[0] * sky_field[0] + sky_field[1] * sky_field[1]


def reference(voltages, calibrated_gain, cells, offsets):
    frame_total = voltages.shape[1]
    antennas = voltages.shape[2]
    channels = voltages.shape[3]
    quiet = jnp.zeros((2, TAPS - 1, antennas, channels), jnp.bfloat16)
    extended = jnp.concatenate([quiet, voltages], axis=1)
    group_size = min(128, antennas)
    groups = antennas // group_size
    stacked = jnp.moveaxis(extended.reshape(2, frame_total + TAPS - 1, groups, group_size, channels), 2, 0)
    gain_groups = jnp.moveaxis(calibrated_gain.reshape(2, groups, group_size, channels), 1, 0)
    volts = lax.map(lambda members: channelize(members[0], members[1], frame_total), (stacked, gain_groups))
    volts = volts.reshape(antennas, 2, frame_total, channels)
    band_width = min(8, channels)
    bands = channels // band_width
    by_band = jnp.moveaxis(volts.reshape(antennas, 2, frame_total, bands, band_width), 3, 0)
    weights, target = footprint(cells, offsets, GRID_CELLS)
    dft_grid = dft_table(GRID_CELLS)

    def image_band(band_volts):
        powers = power_block(band_volts.reshape(antennas, 2, frame_total * band_width), weights, target, GRID_CELLS, dft_grid)
        return powers.reshape(GRID_CELLS, GRID_CELLS, frame_total, band_width).sum(axis=2)

    band_images = lax.map(image_band, by_band)
    band_images = jnp.moveaxis(band_images, 3, 1).reshape(channels, GRID_CELLS, GRID_CELLS)
    return band_images * (1.0 / (antennas * channels * frame_total))
```

```python
import math

import jax
import jax.numpy as jnp
import numpy as np
from jax import lax
from jax.experimental import pallas as pl
from jax.experimental.pallas import tpu as pltpu
from jax.sharding import PartitionSpec as P

GRID = 128
TAPS = 4
FIRST = 8
HALF = GRID // 2
VMEM_BYTES = 48 * 1024 * 1024


def prototype(channels):
    span = TAPS * channels
    places = np.arange(span, dtype=np.float64) + 0.5
    window = 0.54 - 0.46 * np.cos(places * (2.0 * math.pi / span))
    return (np.sinc((places - 0.5 * span) / channels) * window).reshape(TAPS, channels).astype(np.float32)


def twiddle(channels):
    second = channels // FIRST
    phases = (np.arange(FIRST)[:, None] * np.arange(second)[None, :] % channels) * (2.0 * math.pi / channels)
    return np.stack([np.cos(phases), -np.sin(phases)]).astype(np.float32)


def dft_parts(length):
    points = np.arange(length)
    phases = (points[:, None] * points[None, :] % length) * (2.0 * math.pi / length)
    return np.cos(phases), np.sin(phases)


def dft_right(length):
    cosine, sine = dft_parts(length)
    return np.block([[cosine, -sine], [sine, cosine]]).astype(jnp.bfloat16)


def dft_left(length):
    cosine, sine = dft_parts(length)
    return np.block([[cosine, sine], [-sine, cosine]]).astype(jnp.bfloat16)


def eight_points(re, im):
    add = lambda p, q: (p[0] + q[0], p[1] + q[1])
    sub = lambda p, q: (p[0] - q[0], p[1] - q[1])
    sub_i = lambda p, q: (p[0] + q[1], p[1] - q[0])
    add_i = lambda p, q: (p[0] - q[1], p[1] + q[0])
    root = math.sqrt(0.5)
    w = list(zip(re, im))
    a0, a1, a2, a3 = add(w[0], w[4]), sub(w[0], w[4]), add(w[2], w[6]), sub(w[2], w[6])
    a4, a5, a6, a7 = add(w[1], w[5]), sub(w[1], w[5]), add(w[3], w[7]), sub(w[3], w[7])
    b0, b2, b1, b3 = add(a0, a2), sub(a0, a2), sub_i(a1, a3), add_i(a1, a3)
    b4, b6, b5, b7 = add(a4, a6), sub(a4, a6), sub_i(a5, a7), add_i(a5, a7)
    c5 = ((b5[0] + b5[1]) * root, (b5[1] - b5[0]) * root)
    c7 = ((b7[1] - b7[0]) * root, (b7[0] + b7[1]) * -root)
    return [
        add(b0, b4), add(b1, c5), sub_i(b2, b6), add(b3, c7),
        sub(b0, b4), sub(b1, c5), add_i(b2, b6), sub(b3, c7),
    ]


def channelize_kernel(frames, volt_ref, gain_ref, taps_ref, twist_ref, table_ref, out_ref,
                      part_ref, turn_ref, sorted_ref):
    antennas = volt_ref.shape[2]
    channels = volt_ref.shape[3]
    second = channels // FIRST
    spans = frames + TAPS - 1
    both = jnp.concatenate([gain_ref[0], gain_ref[1]], axis=0)
    turn_ref[:, 0 : 2 * antennas] = both.T
    for g in range(spans):
        values = []
        for c in range(2):
            total = None
            for p in range(TAPS):
                f = g - (TAPS - 1) + p
                if 0 <= f < frames:
                    term = volt_ref[c, f].astype(jnp.float32) * taps_ref[p : p + 1, :]
                    total = term if total is None else total + term
            total = total.astype(jnp.bfloat16).astype(jnp.float32)
            values.append([total[:, j * second : (j + 1) * second] for j in range(FIRST)])
        for k, (re, im) in enumerate(eight_points(*values)):
            tw_re = twist_ref[0, k : k + 1, :]
            tw_im = twist_ref[1, k : k + 1, :]
            if k == 0:
                out_re, out_im = re, im
            else:
                out_re = re * tw_re - im * tw_im
                out_im = re * tw_im + im * tw_re
            part_ref[k, g * antennas : (g + 1) * antennas, 0:second] = out_re.astype(jnp.bfloat16)
            part_ref[k, g * antennas : (g + 1) * antennas, second:] = out_im.astype(jnp.bfloat16)
    blank = jnp.zeros(((2 * frames - spans) * antennas, second), jnp.float32)
    for k in range(FIRST):
        spectra = jnp.dot(part_ref[k], table_ref[...], preferred_element_type=jnp.float32)
        gains = turn_ref[pl.ds(k, second, stride=FIRST), 0 : 2 * antennas].T
        gain_re = jnp.concatenate([gains[0:antennas]] * spans, axis=0)
        gain_im = jnp.concatenate([gains[antennas:]] * spans, axis=0)
        re, im = spectra[:, 0:second], spectra[:, second:]
        for c, volts in enumerate((re * gain_re - im * gain_im, re * gain_im + im * gain_re)):
            turned = jnp.concatenate([volts, blank], axis=0).T
            sorted_ref[pl.ds(2 * k + c, second, stride=2 * FIRST), :] = turned
    out_ref[...] = sorted_ref[...].astype(jnp.bfloat16)


def footprint_kernel(cells_ref, offsets_ref, right_ref, left_ref):
    count = cells_ref.shape[1]
    rows, cols = cells_ref[0:1, :], cells_ref[1:2, :]
    share = (offsets_ref[...].astype(jnp.float32) + 0.5) * 0.125
    t_row, t_col = share[0:1, :], share[1:2, :]
    upper = (rows >= HALF).astype(jnp.int32)
    low = rows - upper * HALF
    place = upper * GRID + cols

    def table(height, first, weight):
        at = lax.broadcasted_iota(jnp.int32, (height, count), 0)
        near = jnp.where(at == first, 1.0 - weight, 0.0)
        return jnp.where(at == first + 1, weight, near).astype(jnp.bfloat16)

    right_ref[...] = table(2 * GRID, place, t_col)
    left_ref[...] = table(left_ref.shape[0], low, t_row)


def image_kernel(scale, x_ref, right_ref, left_ref, first_ref, second_ref, out_ref,
                 wide_ref, volt_ref, spread_ref, grid_ref, side_ref, mid_ref):
    blocks = 4
    frames = 4
    antennas = 16
    step = 4 * blocks
    wide_ref[...] = x_ref[...].astype(jnp.float32)
    for kk in range(2):
        for c in range(2):
            tail = None
            for t in range(blocks):
                turned = wide_ref[pl.ds(4 * t + 2 * kk + c, 128, stride=step), :].T
                own = turned[0 : frames * antennas]
                if tail is not None:
                    own = jnp.concatenate(
                        [own[0 : (TAPS - 1) * antennas] + tail, own[(TAPS - 1) * antennas :]], axis=0)
                tail = turned[frames * antennas : (frames + TAPS - 1) * antennas]
                for f in range(frames):
                    volt_ref[kk * blocks + t, 2 * f + c] = own[f * antennas : (f + 1) * antennas]

    out_ref[...] = jnp.zeros_like(out_ref)
    members = 2 * frames

    def chunk(i, carry):
        for a in range(antennas):
            lanes = slice(a * 128, (a + 1) * 128)
            left = left_ref[0:HALF, lanes]
            for m in range(members):
                row = volt_ref[i, m, a : a + 1, :].astype(jnp.bfloat16)
                spread_ref[m * HALF : (m + 1) * HALF, lanes] = left * row
            edge = volt_ref[i, :, a, :]
            edge = jnp.concatenate([edge, edge], axis=0).astype(jnp.bfloat16)
            spread_ref[members * HALF :, lanes] = edge * left_ref[HALF : HALF + 1, lanes]
        grid_ref[...] = lax.dot_general(
            spread_ref[...], right_ref[...], (((1,), (1,)), ((), ())),
            preferred_element_type=jnp.float32)
        for m in range(members):
            grid_ref[m * HALF : m * HALF + 1, GRID:] += grid_ref[
                members * HALF + m : members * HALF + m + 1, 0:GRID]
        for f in range(frames):
            for c in range(2):
                m = 2 * f + c
                for h in range(2):
                    side_ref[f * GRID + h * HALF : f * GRID + (h + 1) * HALF, c * GRID : (c + 1) * GRID] = grid_ref[
                        m * HALF : (m + 1) * HALF, h * GRID : (h + 1) * GRID].astype(jnp.bfloat16)
        half = jnp.dot(side_ref[...], first_ref[...], preferred_element_type=jnp.float32).astype(jnp.bfloat16)
        for f in range(frames):
            for c in range(2):
                mid_ref[c * GRID : (c + 1) * GRID, f * GRID : (f + 1) * GRID] = half[
                    f * GRID : (f + 1) * GRID, c * GRID : (c + 1) * GRID]
        sky = jnp.dot(second_ref[...], mid_ref[...], preferred_element_type=jnp.float32)
        power = sky[0:GRID] * sky[0:GRID] + sky[GRID:] * sky[GRID:]
        total = power[:, 0:GRID]
        for f in range(1, frames):
            total = total + power[:, f * GRID : (f + 1) * GRID]
        out_ref[i // blocks] += total * scale
        return carry

    lax.fori_loop(0, 2 * blocks, chunk, 0)


def whole(shape):
    return pl.BlockSpec(shape, lambda: (0,) * len(shape))


def local(voltages, calibrated_gain, cells, offsets):
    _, frames, antennas, channels = voltages.shape
    second = channels // FIRST
    devices = lax.axis_size("chan") * lax.axis_size("tblk")
    all_antennas = antennas * lax.axis_size("chan")
    scale = 1.0 / (all_antennas * channels * frames * lax.axis_size("tblk"))
    rows = channels * 2

    send = pl.pallas_call(
        lambda *refs: channelize_kernel(frames, *refs),
        out_shape=jax.ShapeDtypeStruct((rows, second), jnp.bfloat16),
        scratch_shapes=[
            pltpu.VMEM((FIRST, (frames + TAPS - 1) * antennas, 2 * second), jnp.bfloat16),
            pltpu.VMEM((channels, 128), jnp.float32),
            pltpu.VMEM((rows, second), jnp.float32),
        ],
        compiler_params=pltpu.CompilerParams(vmem_limit_bytes=VMEM_BYTES),
        name="channelize",
    )(
        voltages, calibrated_gain, jnp.asarray(prototype(channels)),
        jnp.asarray(twiddle(channels)), jnp.asarray(dft_right(second)),
    )

    def by_member(table):
        return table.reshape(2, all_antennas // antennas, antennas).transpose(0, 2, 1).reshape(2, all_antennas)

    right, left = pl.pallas_call(
        footprint_kernel,
        out_shape=(
            jax.ShapeDtypeStruct((2 * GRID, all_antennas), jnp.bfloat16),
            jax.ShapeDtypeStruct((HALF + 16, all_antennas), jnp.bfloat16),
        ),
        compiler_params=pltpu.CompilerParams(vmem_limit_bytes=VMEM_BYTES),
        cost_estimate=pl.CostEstimate(flops=10_000_000, bytes_accessed=1_500_000, transcendentals=0),
        name="footprint",
    )(by_member(cells), by_member(offsets))

    send = send.reshape(devices, rows // devices, second)
    received = lax.all_to_all(send, ("chan", "tblk"), split_axis=0, concat_axis=0, tiled=True)
    received = received.reshape(rows, second)

    members = 2 * frames
    return pl.pallas_call(
        lambda *refs: image_kernel(scale, *refs),
        out_shape=jax.ShapeDtypeStruct((2, GRID, GRID), jnp.float32),
        scratch_shapes=[
            pltpu.VMEM((rows, second), jnp.float32),
            pltpu.VMEM((8, members, antennas, 128), jnp.float32),
            pltpu.VMEM((members * HALF + 16, all_antennas), jnp.bfloat16),
            pltpu.VMEM((members * HALF + 16, 2 * GRID), jnp.float32),
            pltpu.VMEM((frames * GRID, 2 * GRID), jnp.bfloat16),
            pltpu.VMEM((2 * GRID, frames * GRID), jnp.bfloat16),
        ],
        compiler_params=pltpu.CompilerParams(vmem_limit_bytes=VMEM_BYTES),
        name="image",
    )(received, right, left, jnp.asarray(dft_right(GRID)), jnp.asarray(dft_left(GRID)))


def solution(mesh):
    placed = (P(None, "tblk", "chan", None), P(None, "chan", None), P(), P())
    return jax.shard_map(
        local,
        mesh=mesh,
        in_specs=placed,
        out_specs=P(("chan", "tblk"), None, None),
        check_vma=False,
    )
```

```python
import math

import jax
import jax.numpy as jnp
import numpy as np
from jax import lax
from jax.experimental import pallas as pl
from jax.experimental.pallas import tpu as pltpu
from jax.sharding import PartitionSpec as P

GRID = 128
TAPS = 4
FIRST = 8
HALF = GRID // 2
CHUNK = 8
VMEM_BYTES = 32 * 1024 * 1024


def prototype(channels):
    span = TAPS * channels
    places = np.arange(span, dtype=np.float64) + 0.5
    window = 0.54 - 0.46 * np.cos(places * (2.0 * math.pi / span))
    return (np.sinc((places - 0.5 * span) / channels) * window).reshape(TAPS, channels).astype(np.float32)


def twiddle(channels):
    second = channels // FIRST
    phases = (np.arange(FIRST)[:, None] * np.arange(second)[None, :] % channels) * (2.0 * math.pi / channels)
    return np.stack([np.cos(phases), -np.sin(phases)]).astype(np.float32)


def dft_parts(length):
    points = np.arange(length)
    phases = (points[:, None] * points[None, :] % length) * (2.0 * math.pi / length)
    return np.cos(phases), np.sin(phases)


def dft_right(length):
    cosine, sine = dft_parts(length)
    return np.block([[cosine, -sine], [sine, cosine]]).astype(jnp.bfloat16)


def dft_left(length):
    cosine, sine = dft_parts(length)
    return np.block([[cosine, sine], [-sine, cosine]]).astype(jnp.bfloat16)


def eight_points(re, im):
    add = lambda p, q: (p[0] + q[0], p[1] + q[1])
    sub = lambda p, q: (p[0] - q[0], p[1] - q[1])
    sub_i = lambda p, q: (p[0] + q[1], p[1] - q[0])
    add_i = lambda p, q: (p[0] - q[1], p[1] + q[0])
    root = math.sqrt(0.5)
    w = list(zip(re, im))
    a0, a1, a2, a3 = add(w[0], w[4]), sub(w[0], w[4]), add(w[2], w[6]), sub(w[2], w[6])
    a4, a5, a6, a7 = add(w[1], w[5]), sub(w[1], w[5]), add(w[3], w[7]), sub(w[3], w[7])
    b0, b2, b1, b3 = add(a0, a2), sub(a0, a2), sub_i(a1, a3), add_i(a1, a3)
    b4, b6, b5, b7 = add(a4, a6), sub(a4, a6), sub_i(a5, a7), add_i(a5, a7)
    c5 = ((b5[0] + b5[1]) * root, (b5[1] - b5[0]) * root)
    c7 = ((b7[1] - b7[0]) * root, (b7[0] + b7[1]) * -root)
    return [
        add(b0, b4), add(b1, c5), sub_i(b2, b6), add(b3, c7),
        sub(b0, b4), sub(b1, c5), add_i(b2, b6), sub(b3, c7),
    ]


def channelize_kernel(frames, volt_hbm, gain_hbm, taps_hbm, twist_hbm, table_hbm, out_ref,
                      volt_ref, gain_ref, taps_ref, twist_ref, table_ref,
                      part_ref, turn_ref, sorted_ref, sems):
    sources = (volt_hbm, taps_hbm, twist_hbm, gain_hbm, table_hbm)
    targets = (volt_ref, taps_ref, twist_ref, gain_ref, table_ref)
    copies = [pltpu.make_async_copy(s, t, sems.at[i]) for i, (s, t) in enumerate(zip(sources, targets))]
    for copy in copies:
        copy.start()
    antennas = volt_ref.shape[2]
    channels = volt_ref.shape[3]
    second = channels // FIRST
    spans = frames + TAPS - 1
    for copy in copies[0:3]:
        copy.wait()
    for g in range(spans):
        values = []
        for c in range(2):
            total = None
            for p in range(TAPS):
                f = g - (TAPS - 1) + p
                if 0 <= f < frames:
                    term = volt_ref[c, f].astype(jnp.float32) * taps_ref[p : p + 1, :]
                    total = term if total is None else total + term
            total = total.astype(jnp.bfloat16).astype(jnp.float32)
            values.append([total[:, j * second : (j + 1) * second] for j in range(FIRST)])
        for k, (re, im) in enumerate(eight_points(*values)):
            tw_re = twist_ref[0, k : k + 1, :]
            tw_im = twist_ref[1, k : k + 1, :]
            if k == 0:
                out_re, out_im = re, im
            else:
                out_re = re * tw_re - im * tw_im
                out_im = re * tw_im + im * tw_re
            row = (k * spans + g) * antennas
            part_ref[row : row + antennas, 0:second] = out_re.astype(jnp.bfloat16)
            part_ref[row : row + antennas, second:] = out_im.astype(jnp.bfloat16)
    copies[3].wait()
    both = jnp.concatenate([gain_ref[0], gain_ref[1]], axis=0)
    turn_ref[:, 0 : 2 * antennas] = both.T
    copies[4].wait()
    blank = jnp.zeros(((2 * frames - spans) * antennas, second), jnp.float32)
    all_spectra = jnp.dot(part_ref[...], table_ref[...], preferred_element_type=jnp.float32)
    for k in range(FIRST):
        spectra = all_spectra[k * spans * antennas : (k + 1) * spans * antennas]
        gains = turn_ref[pl.ds(k, second, stride=FIRST), 0 : 2 * antennas].T
        gain_re = jnp.concatenate([gains[0:antennas]] * spans, axis=0)
        gain_im = jnp.concatenate([gains[antennas:]] * spans, axis=0)
        re, im = spectra[:, 0:second], spectra[:, second:]
        for c, volts in enumerate((re * gain_re - im * gain_im, re * gain_im + im * gain_re)):
            turned = jnp.concatenate([volts, blank], axis=0).T
            sorted_ref[pl.ds(2 * k + c, second, stride=2 * FIRST), :] = turned
    out_ref[...] = sorted_ref[...].astype(jnp.bfloat16)


def footprint_kernel(cells_ref, offsets_ref, right_ref, left_ref):
    count = cells_ref.shape[1]
    rows, cols = cells_ref[0:1, :], cells_ref[1:2, :]
    share = (offsets_ref[...].astype(jnp.float32) + 0.5) * 0.125
    t_row, t_col = share[0:1, :], share[1:2, :]
    upper = (rows >= HALF).astype(jnp.int32)
    low = rows - upper * HALF
    place = upper * GRID + cols

    def table(height, first, weight):
        at = lax.broadcasted_iota(jnp.int32, (height, count), 0)
        near = jnp.where(at == first, 1.0 - weight, 0.0)
        return jnp.where(at == first + 1, weight, near).astype(jnp.bfloat16)

    right_ref[...] = table(2 * GRID, place, t_col)
    left_ref[...] = table(left_ref.shape[0], low, t_row)


def image_kernel(scale, x_ref, right_ref, left_ref, first_ref, second_ref, out_ref,
                 wide_ref, volt_ref, spread_ref, grid_ref, side_ref):
    blocks = 4
    frames = 4
    antennas = 16
    step = 4 * blocks
    wide_ref[...] = x_ref[...].astype(jnp.float32)
    for kk in range(2):
        for c in range(2):
            tail = None
            for t in range(blocks):
                turned = wide_ref[pl.ds(4 * t + 2 * kk + c, 128, stride=step), :].T
                own = turned[0 : frames * antennas]
                if tail is not None:
                    own = jnp.concatenate(
                        [own[0 : (TAPS - 1) * antennas] + tail, own[(TAPS - 1) * antennas :]], axis=0)
                tail = turned[frames * antennas : (frames + TAPS - 1) * antennas]
                for f in range(frames):
                    row = (kk * blocks + t) * frames + f
                    volt_ref[row // CHUNK, 2 * (row % CHUNK) + c] = own[f * antennas : (f + 1) * antennas]

    members = 2 * CHUNK

    def chunk(i, carry):
        for a in range(antennas):
            lanes = slice(a * 128, (a + 1) * 128)
            left = left_ref[0:HALF, lanes]
            for m in range(members):
                row = volt_ref[i, m, a : a + 1, :].astype(jnp.bfloat16)
                spread_ref[m * HALF : (m + 1) * HALF, lanes] = left * row
            edge = volt_ref[i, :, a, :].astype(jnp.bfloat16)
            spread_ref[members * HALF :, lanes] = edge * left_ref[HALF : HALF + 1, lanes]
        grid_ref[...] = lax.dot_general(
            spread_ref[...], right_ref[...], (((1,), (1,)), ((), ())),
            preferred_element_type=jnp.float32)
        for m in range(members):
            grid_ref[m * HALF : m * HALF + 1, GRID:] += grid_ref[
                members * HALF + m : members * HALF + m + 1, 0:GRID]
        for f in range(CHUNK):
            for c in range(2):
                m = 2 * f + c
                for h in range(2):
                    side_ref[i * CHUNK + f, h * HALF : (h + 1) * HALF, c * GRID : (c + 1) * GRID] = grid_ref[
                        m * HALF : (m + 1) * HALF, h * GRID : (h + 1) * GRID].astype(jnp.bfloat16)
        return carry

    lax.fori_loop(0, 2 * blocks * frames // CHUNK, chunk, 0)
    for kk in range(2):
        total = None
        for t in range(blocks):
            first = (kk * blocks + t) * frames
            side = side_ref[first : first + frames].reshape(frames * GRID, 2 * GRID)
            half = jnp.dot(side, first_ref[...], preferred_element_type=jnp.float32).astype(jnp.bfloat16)
            mid = jnp.concatenate([
                jnp.concatenate([
                    half[f * GRID : (f + 1) * GRID, c * GRID : (c + 1) * GRID] for f in range(frames)], axis=1)
                for c in range(2)], axis=0)
            sky = jnp.dot(second_ref[...], mid, preferred_element_type=jnp.float32)
            power = sky[0:GRID] * sky[0:GRID] + sky[GRID:] * sky[GRID:]
            for f in range(frames):
                part = power[:, f * GRID : (f + 1) * GRID]
                total = part if total is None else total + part
        out_ref[kk] = total * scale


def local(voltages, calibrated_gain, cells, offsets):
    _, frames, antennas, channels = voltages.shape
    second = channels // FIRST
    devices = lax.axis_size("chan") * lax.axis_size("tblk")
    all_antennas = antennas * lax.axis_size("chan")
    scale = 1.0 / (all_antennas * channels * frames * lax.axis_size("tblk"))
    rows = channels * 2

    send = pl.pallas_call(
        lambda *refs: channelize_kernel(frames, *refs),
        out_shape=jax.ShapeDtypeStruct((rows, second), jnp.bfloat16),
        in_specs=[pl.BlockSpec(memory_space=pl.ANY)] * 5,
        scratch_shapes=[
            pltpu.VMEM(voltages.shape, jnp.bfloat16),
            pltpu.VMEM(calibrated_gain.shape, jnp.float32),
            pltpu.VMEM((TAPS, channels), jnp.float32),
            pltpu.VMEM((2, FIRST, second), jnp.float32),
            pltpu.VMEM((2 * second, 2 * second), jnp.bfloat16),
            pltpu.VMEM((FIRST * (frames + TAPS - 1) * antennas, 2 * second), jnp.bfloat16),
            pltpu.VMEM((channels, 128), jnp.float32),
            pltpu.VMEM((rows, second), jnp.float32),
            pltpu.SemaphoreType.DMA((5,)),
        ],
        compiler_params=pltpu.CompilerParams(vmem_limit_bytes=60 * 1024 * 1024),
        name="channelize",
    )(
        voltages, calibrated_gain, jnp.asarray(prototype(channels)),
        jnp.asarray(twiddle(channels)), jnp.asarray(dft_right(second)),
    )

    def by_member(table):
        return table.reshape(2, all_antennas // antennas, antennas).transpose(0, 2, 1).reshape(2, all_antennas)

    right, left = pl.pallas_call(
        footprint_kernel,
        out_shape=(
            jax.ShapeDtypeStruct((2 * GRID, all_antennas), jnp.bfloat16),
            jax.ShapeDtypeStruct((HALF + 16, all_antennas), jnp.bfloat16),
        ),
        compiler_params=pltpu.CompilerParams(vmem_limit_bytes=VMEM_BYTES),
        cost_estimate=pl.CostEstimate(flops=10_000_000, bytes_accessed=1_500_000, transcendentals=0),
        name="footprint",
    )(by_member(cells), by_member(offsets))

    send = send.reshape(devices, rows // devices, second)
    received = lax.all_to_all(send, ("chan", "tblk"), split_axis=0, concat_axis=0, tiled=True)
    received = received.reshape(rows, second)

    members = 2 * CHUNK
    chunks = 2 * frames * lax.axis_size("tblk") // CHUNK
    return pl.pallas_call(
        lambda *refs: image_kernel(scale, *refs),
        out_shape=jax.ShapeDtypeStruct((2, GRID, GRID), jnp.float32),
        scratch_shapes=[
            pltpu.VMEM((rows, second), jnp.float32),
            pltpu.VMEM((chunks, members, antennas, 128), jnp.float32),
            pltpu.VMEM((members * HALF + 16, all_antennas), jnp.bfloat16),
            pltpu.VMEM((members * HALF + 16, 2 * GRID), jnp.float32),
            pltpu.VMEM((chunks * CHUNK, GRID, 2 * GRID), jnp.bfloat16),
        ],
        compiler_params=pltpu.CompilerParams(vmem_limit_bytes=VMEM_BYTES),
        name="image",
    )(received, right, left, jnp.asarray(dft_right(GRID)), jnp.asarray(dft_left(GRID)))


def solution(mesh):
    placed = (P(None, "tblk", "chan", None), P(None, "chan", None), P(), P())
    return jax.shard_map(
        local,
        mesh=mesh,
        in_specs=placed,
        out_specs=P(("chan", "tblk"), None, None),
        check_vma=False,
    )
```

```python
import math

import jax
import jax.numpy as jnp
import numpy as np
from jax import lax
from jax.experimental import pallas as pl
from jax.experimental.pallas import tpu as pltpu
from jax.sharding import PartitionSpec as P

GRID = 128
TAPS = 4
FIRST = 8
BANDS = 4
BAND = GRID // BANDS
CHUNK = 16
VMEM_BYTES = 32 * 1024 * 1024


def prototype(channels):
    span = TAPS * channels
    places = np.arange(span, dtype=np.float64) + 0.5
    window = 0.54 - 0.46 * np.cos(places * (2.0 * math.pi / span))
    return (np.sinc((places - 0.5 * span) / channels) * window).reshape(TAPS, channels).astype(np.float32)


def twiddle(channels):
    second = channels // FIRST
    phases = (np.arange(FIRST)[:, None] * np.arange(second)[None, :] % channels) * (2.0 * math.pi / channels)
    return np.stack([np.cos(phases), -np.sin(phases)]).astype(np.float32)


def dft_parts(length):
    points = np.arange(length)
    phases = (points[:, None] * points[None, :] % length) * (2.0 * math.pi / length)
    return np.cos(phases), np.sin(phases)


def dft_right(length):
    cosine, sine = dft_parts(length)
    return np.block([[cosine, -sine], [sine, cosine]]).astype(jnp.bfloat16)


def dft_left(length):
    cosine, sine = dft_parts(length)
    return np.block([[cosine, sine], [-sine, cosine]]).astype(jnp.bfloat16)


def eight_points(re, im):
    add = lambda p, q: (p[0] + q[0], p[1] + q[1])
    sub = lambda p, q: (p[0] - q[0], p[1] - q[1])
    sub_i = lambda p, q: (p[0] + q[1], p[1] - q[0])
    add_i = lambda p, q: (p[0] - q[1], p[1] + q[0])
    root = math.sqrt(0.5)
    w = list(zip(re, im))
    a0, a1, a2, a3 = add(w[0], w[4]), sub(w[0], w[4]), add(w[2], w[6]), sub(w[2], w[6])
    a4, a5, a6, a7 = add(w[1], w[5]), sub(w[1], w[5]), add(w[3], w[7]), sub(w[3], w[7])
    b0, b2, b1, b3 = add(a0, a2), sub(a0, a2), sub_i(a1, a3), add_i(a1, a3)
    b4, b6, b5, b7 = add(a4, a6), sub(a4, a6), sub_i(a5, a7), add_i(a5, a7)
    c5 = ((b5[0] + b5[1]) * root, (b5[1] - b5[0]) * root)
    c7 = ((b7[1] - b7[0]) * root, (b7[0] + b7[1]) * -root)
    return [
        add(b0, b4), add(b1, c5), sub_i(b2, b6), add(b3, c7),
        sub(b0, b4), sub(b1, c5), add_i(b2, b6), sub(b3, c7),
    ]


def channelize_kernel(frames, volt_hbm, gain_hbm, taps_hbm, twist_hbm, table_hbm, out_ref,
                      volt_ref, gain_ref, taps_ref, twist_ref, table_ref,
                      part_ref, turn_ref, sorted_ref, sems):
    sources = (volt_hbm, taps_hbm, twist_hbm, gain_hbm, table_hbm)
    targets = (volt_ref, taps_ref, twist_ref, gain_ref, table_ref)
    copies = [pltpu.make_async_copy(s, t, sems.at[i]) for i, (s, t) in enumerate(zip(sources, targets))]
    for copy in copies:
        copy.start()
    antennas = volt_ref.shape[2]
    channels = volt_ref.shape[3]
    second = channels // FIRST
    spans = frames + TAPS - 1
    for copy in copies[0:3]:
        copy.wait()
    for g in range(spans):
        values = []
        for c in range(2):
            total = None
            for p in range(TAPS):
                f = g - (TAPS - 1) + p
                if 0 <= f < frames:
                    term = volt_ref[c, f].astype(jnp.float32) * taps_ref[p : p + 1, :]
                    total = term if total is None else total + term
            total = total.astype(jnp.bfloat16).astype(jnp.float32)
            values.append([total[:, j * second : (j + 1) * second] for j in range(FIRST)])
        for k, (re, im) in enumerate(eight_points(*values)):
            tw_re = twist_ref[0, k : k + 1, :]
            tw_im = twist_ref[1, k : k + 1, :]
            if k == 0:
                out_re, out_im = re, im
            else:
                out_re = re * tw_re - im * tw_im
                out_im = re * tw_im + im * tw_re
            row = (k * spans + g) * antennas
            part_ref[row : row + antennas, 0:second] = out_re.astype(jnp.bfloat16)
            part_ref[row : row + antennas, second:] = out_im.astype(jnp.bfloat16)
    copies[3].wait()
    both = jnp.concatenate([gain_ref[0], gain_ref[1]], axis=0)
    turn_ref[:, 0 : 2 * antennas] = both.T
    copies[4].wait()
    blank = jnp.zeros(((2 * frames - spans) * antennas, second), jnp.float32)
    all_spectra = jnp.dot(part_ref[...], table_ref[...], preferred_element_type=jnp.float32)
    for k in range(FIRST):
        spectra = all_spectra[k * spans * antennas : (k + 1) * spans * antennas]
        gains = turn_ref[pl.ds(k, second, stride=FIRST), 0 : 2 * antennas].T
        gain_re = jnp.concatenate([gains[0:antennas]] * spans, axis=0)
        gain_im = jnp.concatenate([gains[antennas:]] * spans, axis=0)
        re, im = spectra[:, 0:second], spectra[:, second:]
        for c, volts in enumerate((re * gain_re - im * gain_im, re * gain_im + im * gain_re)):
            turned = jnp.concatenate([volts, blank], axis=0).T
            sorted_ref[pl.ds(2 * k + c, second, stride=2 * FIRST), :] = turned
    out_ref[...] = sorted_ref[...].astype(jnp.bfloat16)


def footprint_kernel(cells_ref, offsets_ref, right_ref, left_ref):
    count = cells_ref.shape[1]
    rows, cols = cells_ref[0:1, :], cells_ref[1:2, :]
    share = (offsets_ref[...].astype(jnp.float32) + 0.5) * 0.125
    t_row, t_col = share[0:1, :], share[1:2, :]
    low = rows & (BAND - 1)
    place = (rows - low) * (GRID // BAND) + cols

    def table(height, first, weight):
        at = lax.broadcasted_iota(jnp.int32, (height, count), 0)
        near = jnp.where(at == first, 1.0 - weight, 0.0)
        return jnp.where(at == first + 1, weight, near).astype(jnp.bfloat16)

    right_ref[...] = table(BANDS * GRID, place, t_col)
    left_ref[...] = table(left_ref.shape[0], low, t_row)


def image_kernel(scale, x_ref, right_ref, left_ref, first_ref, second_ref, out_ref,
                 wide_ref, volt_ref, spread_ref, grid_ref, side_ref):
    blocks = 4
    frames = 4
    antennas = 16
    step = 4 * blocks
    wide_ref[...] = x_ref[...].astype(jnp.float32)
    for kk in range(2):
        for c in range(2):
            tail = None
            for t in range(blocks):
                turned = wide_ref[pl.ds(4 * t + 2 * kk + c, 128, stride=step), :].T
                own = turned[0 : frames * antennas]
                if tail is not None:
                    own = jnp.concatenate(
                        [own[0 : (TAPS - 1) * antennas] + tail, own[(TAPS - 1) * antennas :]], axis=0)
                tail = turned[frames * antennas : (frames + TAPS - 1) * antennas]
                for f in range(frames):
                    row = (kk * blocks + t) * frames + f
                    volt_ref[row // CHUNK, 2 * (row % CHUNK) + c] = own[f * antennas : (f + 1) * antennas]

    members = 2 * CHUNK

    def chunk(i, carry):
        for a in range(antennas):
            lanes = slice(a * 128, (a + 1) * 128)
            left = left_ref[0:BAND, lanes]
            for m in range(members):
                row = volt_ref[i, m, a : a + 1, :].astype(jnp.bfloat16)
                spread_ref[m * BAND : (m + 1) * BAND, lanes] = left * row
            edge = volt_ref[i, :, a, :].astype(jnp.bfloat16)
            spread_ref[members * BAND :, lanes] = edge * left_ref[BAND : BAND + 1, lanes]
        grid_ref[...] = lax.dot_general(
            spread_ref[...], right_ref[...], (((1,), (1,)), ((), ())),
            preferred_element_type=jnp.float32)
        for m in range(members):
            grid_ref[m * BAND : m * BAND + 1, GRID:] += grid_ref[
                members * BAND + m : members * BAND + m + 1, : (BANDS - 1) * GRID]
        for f in range(CHUNK):
            for c in range(2):
                m = 2 * f + c
                for h in range(BANDS):
                    side_ref[i * CHUNK + f, h * BAND : (h + 1) * BAND, c * GRID : (c + 1) * GRID] = grid_ref[
                        m * BAND : (m + 1) * BAND, h * GRID : (h + 1) * GRID].astype(jnp.bfloat16)
        return carry

    lax.fori_loop(0, 2 * blocks * frames // CHUNK, chunk, 0)
    for kk in range(2):
        total = None
        for t in range(blocks):
            first = (kk * blocks + t) * frames
            side = side_ref[first : first + frames].reshape(frames * GRID, 2 * GRID)
            half = jnp.dot(side, first_ref[...], preferred_element_type=jnp.float32).astype(jnp.bfloat16)
            mid = jnp.concatenate([
                jnp.concatenate([
                    half[f * GRID : (f + 1) * GRID, c * GRID : (c + 1) * GRID] for f in range(frames)], axis=1)
                for c in range(2)], axis=0)
            sky = jnp.dot(second_ref[...], mid, preferred_element_type=jnp.float32)
            power = sky[0:GRID] * sky[0:GRID] + sky[GRID:] * sky[GRID:]
            for f in range(frames):
                part = power[:, f * GRID : (f + 1) * GRID]
                total = part if total is None else total + part
        out_ref[kk] = total * scale


def local(voltages, calibrated_gain, cells, offsets):
    _, frames, antennas, channels = voltages.shape
    second = channels // FIRST
    devices = lax.axis_size("chan") * lax.axis_size("tblk")
    all_antennas = antennas * lax.axis_size("chan")
    scale = 1.0 / (all_antennas * channels * frames * lax.axis_size("tblk"))
    rows = channels * 2

    send = pl.pallas_call(
        lambda *refs: channelize_kernel(frames, *refs),
        out_shape=jax.ShapeDtypeStruct((rows, second), jnp.bfloat16),
        in_specs=[pl.BlockSpec(memory_space=pl.ANY)] * 5,
        scratch_shapes=[
            pltpu.VMEM(voltages.shape, jnp.bfloat16),
            pltpu.VMEM(calibrated_gain.shape, jnp.float32),
            pltpu.VMEM((TAPS, channels), jnp.float32),
            pltpu.VMEM((2, FIRST, second), jnp.float32),
            pltpu.VMEM((2 * second, 2 * second), jnp.bfloat16),
            pltpu.VMEM((FIRST * (frames + TAPS - 1) * antennas, 2 * second), jnp.bfloat16),
            pltpu.VMEM((channels, 128), jnp.float32),
            pltpu.VMEM((rows, second), jnp.float32),
            pltpu.SemaphoreType.DMA((5,)),
        ],
        compiler_params=pltpu.CompilerParams(vmem_limit_bytes=60 * 1024 * 1024),
        name="channelize",
    )(
        voltages, calibrated_gain, jnp.asarray(prototype(channels)),
        jnp.asarray(twiddle(channels)), jnp.asarray(dft_right(second)),
    )

    def by_member(table):
        return table.reshape(2, all_antennas // antennas, antennas).transpose(0, 2, 1).reshape(2, all_antennas)

    right, left = pl.pallas_call(
        footprint_kernel,
        out_shape=(
            jax.ShapeDtypeStruct((BANDS * GRID, all_antennas), jnp.bfloat16),
            jax.ShapeDtypeStruct((BAND + 16, all_antennas), jnp.bfloat16),
        ),
        compiler_params=pltpu.CompilerParams(vmem_limit_bytes=VMEM_BYTES),
        cost_estimate=pl.CostEstimate(flops=10_000_000, bytes_accessed=1_500_000, transcendentals=0),
        name="footprint",
    )(by_member(cells), by_member(offsets))

    send = send.reshape(devices, rows // devices, second)
    received = lax.all_to_all(send, ("chan", "tblk"), split_axis=0, concat_axis=0, tiled=True)
    received = received.reshape(rows, second)

    members = 2 * CHUNK
    chunks = 2 * frames * lax.axis_size("tblk") // CHUNK
    return pl.pallas_call(
        lambda *refs: image_kernel(scale, *refs),
        out_shape=jax.ShapeDtypeStruct((2, GRID, GRID), jnp.float32),
        scratch_shapes=[
            pltpu.VMEM((rows, second), jnp.float32),
            pltpu.VMEM((chunks, members, antennas, 128), jnp.float32),
            pltpu.VMEM((members * (BAND + 1), all_antennas), jnp.bfloat16),
            pltpu.VMEM((members * (BAND + 1), BANDS * GRID), jnp.float32),
            pltpu.VMEM((chunks * CHUNK, GRID, 2 * GRID), jnp.bfloat16),
        ],
        compiler_params=pltpu.CompilerParams(vmem_limit_bytes=VMEM_BYTES),
        name="image",
    )(received, right, left, jnp.asarray(dft_right(GRID)), jnp.asarray(dft_left(GRID)))


def solution(mesh):
    placed = (P(None, "tblk", "chan", None), P(None, "chan", None), P(), P())
    return jax.shard_map(
        local,
        mesh=mesh,
        in_specs=placed,
        out_specs=P(("chan", "tblk"), None, None),
        check_vma=False,
    )
```

```python
import math

import jax
import jax.numpy as jnp
import numpy as np
from jax import lax
from jax.experimental import pallas as pl
from jax.experimental.pallas import tpu as pltpu
from jax.sharding import PartitionSpec as P

GRID = 128
TAPS = 4
FIRST = 8
BANDS = 4
BAND = GRID // BANDS
GROUP = 8
CHUNK = 16
VMEM_BYTES = 32 * 1024 * 1024


def prototype(channels):
    span = TAPS * channels
    places = np.arange(span, dtype=np.float64) + 0.5
    window = 0.54 - 0.46 * np.cos(places * (2.0 * math.pi / span))
    return (np.sinc((places - 0.5 * span) / channels) * window).reshape(TAPS, channels).astype(np.float32)


def twiddle(channels):
    second = channels // FIRST
    phases = (np.arange(FIRST)[:, None] * np.arange(second)[None, :] % channels) * (2.0 * math.pi / channels)
    return np.stack([np.cos(phases), -np.sin(phases)]).astype(np.float32)


def dft_parts(length):
    points = np.arange(length)
    phases = (points[:, None] * points[None, :] % length) * (2.0 * math.pi / length)
    return np.cos(phases), np.sin(phases)


def dft_right(length):
    cosine, sine = dft_parts(length)
    return np.block([[cosine, -sine], [sine, cosine]]).astype(jnp.bfloat16)


def dft_left(length):
    cosine, sine = dft_parts(length)
    return np.block([[cosine, sine], [-sine, cosine]]).astype(jnp.bfloat16)


def eight_points(re, im):
    add = lambda p, q: (p[0] + q[0], p[1] + q[1])
    sub = lambda p, q: (p[0] - q[0], p[1] - q[1])
    sub_i = lambda p, q: (p[0] + q[1], p[1] - q[0])
    add_i = lambda p, q: (p[0] - q[1], p[1] + q[0])
    root = math.sqrt(0.5)
    w = list(zip(re, im))
    a0, a1, a2, a3 = add(w[0], w[4]), sub(w[0], w[4]), add(w[2], w[6]), sub(w[2], w[6])
    a4, a5, a6, a7 = add(w[1], w[5]), sub(w[1], w[5]), add(w[3], w[7]), sub(w[3], w[7])
    b0, b2, b1, b3 = add(a0, a2), sub(a0, a2), sub_i(a1, a3), add_i(a1, a3)
    b4, b6, b5, b7 = add(a4, a6), sub(a4, a6), sub_i(a5, a7), add_i(a5, a7)
    c5 = ((b5[0] + b5[1]) * root, (b5[1] - b5[0]) * root)
    c7 = ((b7[1] - b7[0]) * root, (b7[0] + b7[1]) * -root)
    return [
        add(b0, b4), add(b1, c5), sub_i(b2, b6), add(b3, c7),
        sub(b0, b4), sub(b1, c5), add_i(b2, b6), sub(b3, c7),
    ]


def channelize_kernel(frames, volt_hbm, gain_hbm, taps_hbm, twist_hbm, table_hbm, out_ref,
                      volt_ref, gain_ref, taps_ref, twist_ref, table_ref,
                      part_ref, turn_ref, sorted_ref, sems):
    sources = (volt_hbm, taps_hbm, twist_hbm, gain_hbm, table_hbm)
    targets = (volt_ref, taps_ref, twist_ref, gain_ref, table_ref)
    copies = [pltpu.make_async_copy(s, t, sems.at[i]) for i, (s, t) in enumerate(zip(sources, targets))]
    for copy in copies:
        copy.start()
    antennas = volt_ref.shape[2]
    channels = volt_ref.shape[3]
    second = channels // FIRST
    spans = frames + TAPS - 1
    for copy in copies[0:3]:
        copy.wait()
    for g in range(spans):
        values = []
        for c in range(2):
            total = None
            for p in range(TAPS):
                f = g - (TAPS - 1) + p
                if 0 <= f < frames:
                    term = volt_ref[c, f].astype(jnp.float32) * taps_ref[p : p + 1, :]
                    total = term if total is None else total + term
            total = total.astype(jnp.bfloat16).astype(jnp.float32)
            values.append([total[:, j * second : (j + 1) * second] for j in range(FIRST)])
        for k, (re, im) in enumerate(eight_points(*values)):
            tw_re = twist_ref[0, k : k + 1, :]
            tw_im = twist_ref[1, k : k + 1, :]
            if k == 0:
                out_re, out_im = re, im
            else:
                out_re = re * tw_re - im * tw_im
                out_im = re * tw_im + im * tw_re
            row = (k * spans + g) * antennas
            part_ref[row : row + antennas, 0:second] = out_re.astype(jnp.bfloat16)
            part_ref[row : row + antennas, second:] = out_im.astype(jnp.bfloat16)
    copies[3].wait()
    both = jnp.concatenate([gain_ref[0], gain_ref[1]], axis=0)
    turn_ref[0:channels, 0 : 2 * antennas] = both.T
    copies[4].wait()
    blank = jnp.zeros(((2 * frames - spans) * antennas, second), jnp.float32)
    all_spectra = jnp.dot(part_ref[...], table_ref[...], preferred_element_type=jnp.float32)
    for k in range(FIRST):
        spectra = all_spectra[k * spans * antennas : (k + 1) * spans * antennas]
        gains = turn_ref[pl.ds(k, second, stride=FIRST), 0 : 2 * antennas].T
        gain_re = jnp.concatenate([gains[0:antennas]] * spans, axis=0)
        gain_im = jnp.concatenate([gains[antennas:]] * spans, axis=0)
        re, im = spectra[:, 0:second], spectra[:, second:]
        for c, volts in enumerate((re * gain_re - im * gain_im, re * gain_im + im * gain_re)):
            turned = jnp.concatenate([volts, blank], axis=0).T
            sorted_ref[pl.ds(2 * k + c, second, stride=2 * FIRST), :] = turned
    out_ref[...] = sorted_ref[0 : out_ref.shape[0]].astype(jnp.bfloat16)


def footprint_kernel(cells_ref, offsets_ref, right_ref, left_ref):
    count = cells_ref.shape[1]
    rows, cols = cells_ref[0:1, :], cells_ref[1:2, :]
    share = (offsets_ref[...].astype(jnp.float32) + 0.5) * 0.125
    t_row, t_col = share[0:1, :], share[1:2, :]
    low = rows & (BAND - 1)
    place = (rows - low) * (GRID // BAND) + cols

    def table(height, first, weight):
        at = lax.broadcasted_iota(jnp.int32, (height, count), 0)
        near = jnp.where(at == first, 1.0 - weight, 0.0)
        return jnp.where(at == first + 1, weight, near).astype(jnp.bfloat16)

    right_ref[...] = table(BANDS * GRID, place, t_col)
    left_ref[...] = table(left_ref.shape[0], low, t_row)


def image_kernel(scale, x_ref, right_ref, left_ref, first_ref, second_ref, out_ref,
                 wide_ref, volt_ref, spread_ref, grid_ref, side_ref):
    blocks = 4
    frames = 4
    antennas = 16
    step = 4 * blocks
    wide_ref[0 : x_ref.shape[0]] = x_ref[...].astype(jnp.float32)
    for kk in range(2):
        for c in range(2):
            tail = None
            for t in range(blocks):
                turned = wide_ref[pl.ds(4 * t + 2 * kk + c, 128, stride=step), :].T
                own = turned[0 : frames * antennas]
                if tail is not None:
                    own = jnp.concatenate(
                        [own[0 : (TAPS - 1) * antennas] + tail, own[(TAPS - 1) * antennas :]], axis=0)
                tail = turned[frames * antennas : (frames + TAPS - 1) * antennas]
                for f in range(frames):
                    row = (kk * blocks + t) * frames + f
                    volt_ref[row // CHUNK, 2 * (row % CHUNK) + c] = own[f * antennas : (f + 1) * antennas]

    members = 2 * CHUNK

    def chunk(i, carry):
        for a in range(antennas):
            lanes = slice(a * 128, (a + 1) * 128)
            left = left_ref[0:BAND, lanes]
            for m in range(members):
                row = volt_ref[i, m, a : a + 1, :].astype(jnp.bfloat16)
                spread_ref[m * BAND : (m + 1) * BAND, lanes] = left * row
            edge = volt_ref[i, :, a, :].astype(jnp.bfloat16)
            spread_ref[members * BAND :, lanes] = edge * left_ref[BAND : BAND + 1, lanes]
        grid_ref[...] = lax.dot_general(
            spread_ref[...], right_ref[...], (((1,), (1,)), ((), ())),
            preferred_element_type=jnp.float32)
        for m in range(members):
            grid_ref[m * BAND : m * BAND + 1, GRID:] += grid_ref[
                members * BAND + m : members * BAND + m + 1, : (BANDS - 1) * GRID]
        for f in range(CHUNK):
            for c in range(2):
                m = 2 * f + c
                for h in range(BANDS):
                    side_ref[i * CHUNK + f, h * BAND : (h + 1) * BAND, c * GRID : (c + 1) * GRID] = grid_ref[
                        m * BAND : (m + 1) * BAND, h * GRID : (h + 1) * GRID].astype(jnp.bfloat16)
        return carry

    lax.fori_loop(0, 2 * blocks * frames // CHUNK, chunk, 0)
    for kk in range(2):
        total = None
        for t in range(0, blocks * frames, GROUP):
            first = kk * blocks * frames + t
            side = side_ref[first : first + GROUP].reshape(GROUP * GRID, 2 * GRID)
            half = jnp.dot(side, first_ref[...], preferred_element_type=jnp.float32).astype(jnp.bfloat16)
            mid = jnp.concatenate([
                jnp.concatenate([
                    half[f * GRID : (f + 1) * GRID, c * GRID : (c + 1) * GRID] for f in range(GROUP)], axis=1)
                for c in range(2)], axis=0)
            sky = jnp.dot(second_ref[...], mid, preferred_element_type=jnp.float32)
            power = sky[0:GRID] * sky[0:GRID] + sky[GRID:] * sky[GRID:]
            for f in range(GROUP):
                part = power[:, f * GRID : (f + 1) * GRID]
                total = part if total is None else total + part
        out_ref[kk] = total * scale


def local(voltages, calibrated_gain, cells, offsets):
    _, frames, antennas, channels = voltages.shape
    second = channels // FIRST
    devices = lax.axis_size("chan") * lax.axis_size("tblk")
    all_antennas = antennas * lax.axis_size("chan")
    scale = 1.0 / (all_antennas * channels * frames * lax.axis_size("tblk"))
    rows = channels * 2

    send = pl.pallas_call(
        lambda *refs: channelize_kernel(frames, *refs),
        out_shape=jax.ShapeDtypeStruct((rows, second), jnp.bfloat16),
        in_specs=[pl.BlockSpec(memory_space=pl.ANY)] * 5,
        scratch_shapes=[
            pltpu.VMEM(voltages.shape, jnp.bfloat16),
            pltpu.VMEM(calibrated_gain.shape, jnp.float32),
            pltpu.VMEM((TAPS, channels), jnp.float32),
            pltpu.VMEM((2, FIRST, second), jnp.float32),
            pltpu.VMEM((2 * second, 2 * second), jnp.bfloat16),
            pltpu.VMEM((FIRST * (frames + TAPS - 1) * antennas, 2 * second), jnp.bfloat16),
            pltpu.VMEM((channels + FIRST, 128), jnp.float32),
            pltpu.VMEM((rows + 2 * FIRST, second), jnp.float32),
            pltpu.SemaphoreType.DMA((5,)),
        ],
        compiler_params=pltpu.CompilerParams(vmem_limit_bytes=60 * 1024 * 1024),
        name="channelize",
    )(
        voltages, calibrated_gain, jnp.asarray(prototype(channels)),
        jnp.asarray(twiddle(channels)), jnp.asarray(dft_right(second)),
    )

    def by_member(table):
        return table.reshape(2, all_antennas // antennas, antennas).transpose(0, 2, 1).reshape(2, all_antennas)

    right, left = pl.pallas_call(
        footprint_kernel,
        out_shape=(
            jax.ShapeDtypeStruct((BANDS * GRID, all_antennas), jnp.bfloat16),
            jax.ShapeDtypeStruct((BAND + 16, all_antennas), jnp.bfloat16),
        ),
        compiler_params=pltpu.CompilerParams(vmem_limit_bytes=VMEM_BYTES),
        cost_estimate=pl.CostEstimate(flops=10_000_000, bytes_accessed=1_500_000, transcendentals=0),
        name="footprint",
    )(by_member(cells), by_member(offsets))

    send = send.reshape(devices, rows // devices, second)
    received = lax.all_to_all(send, ("chan", "tblk"), split_axis=0, concat_axis=0, tiled=True)
    received = received.reshape(rows, second)

    members = 2 * CHUNK
    chunks = 2 * frames * lax.axis_size("tblk") // CHUNK
    return pl.pallas_call(
        lambda *refs: image_kernel(scale, *refs),
        out_shape=jax.ShapeDtypeStruct((2, GRID, GRID), jnp.float32),
        scratch_shapes=[
            pltpu.VMEM((rows + 16, second), jnp.float32),
            pltpu.VMEM((chunks, members, antennas, 128), jnp.float32),
            pltpu.VMEM((members * (BAND + 1), all_antennas), jnp.bfloat16),
            pltpu.VMEM((members * (BAND + 1), BANDS * GRID), jnp.float32),
            pltpu.VMEM((chunks * CHUNK, GRID, 2 * GRID), jnp.bfloat16),
        ],
        compiler_params=pltpu.CompilerParams(vmem_limit_bytes=VMEM_BYTES),
        name="image",
    )(received, right, left, jnp.asarray(dft_right(GRID)), jnp.asarray(dft_left(GRID)))


def solution(mesh):
    placed = (P(None, "tblk", "chan", None), P(None, "chan", None), P(), P())
    return jax.shard_map(
        local,
        mesh=mesh,
        in_specs=placed,
        out_specs=P(("chan", "tblk"), None, None),
        check_vma=False,
    )
```

```python
import math

import jax
import jax.numpy as jnp
import numpy as np
from jax import lax
from jax.experimental import pallas as pl
from jax.experimental.pallas import tpu as pltpu
from jax.sharding import PartitionSpec as P

GRID = 128
TAPS = 4
FIRST = 8
BANDS = 4
BAND = GRID // BANDS
OUT_PITCH = 24
IN_PITCH = 17
GROUP = 8
CHUNK = 16
VMEM_BYTES = 32 * 1024 * 1024


def prototype(channels):
    span = TAPS * channels
    places = np.arange(span, dtype=np.float64) + 0.5
    window = 0.54 - 0.46 * np.cos(places * (2.0 * math.pi / span))
    return (np.sinc((places - 0.5 * span) / channels) * window).reshape(TAPS, channels).astype(np.float32)


def twiddle(channels):
    second = channels // FIRST
    phases = (np.arange(FIRST)[:, None] * np.arange(second)[None, :] % channels) * (2.0 * math.pi / channels)
    return np.stack([np.cos(phases), -np.sin(phases)]).astype(np.float32)


def dft_parts(length):
    points = np.arange(length)
    phases = (points[:, None] * points[None, :] % length) * (2.0 * math.pi / length)
    return np.cos(phases), np.sin(phases)


def dft_right(length):
    cosine, sine = dft_parts(length)
    return np.block([[cosine, -sine], [sine, cosine]]).astype(jnp.bfloat16)


def dft_left(length):
    cosine, sine = dft_parts(length)
    return np.block([[cosine, sine], [-sine, cosine]]).astype(jnp.bfloat16)


def eight_points(re, im):
    add = lambda p, q: (p[0] + q[0], p[1] + q[1])
    sub = lambda p, q: (p[0] - q[0], p[1] - q[1])
    sub_i = lambda p, q: (p[0] + q[1], p[1] - q[0])
    add_i = lambda p, q: (p[0] - q[1], p[1] + q[0])
    root = math.sqrt(0.5)
    w = list(zip(re, im))
    a0, a1, a2, a3 = add(w[0], w[4]), sub(w[0], w[4]), add(w[2], w[6]), sub(w[2], w[6])
    a4, a5, a6, a7 = add(w[1], w[5]), sub(w[1], w[5]), add(w[3], w[7]), sub(w[3], w[7])
    b0, b2, b1, b3 = add(a0, a2), sub(a0, a2), sub_i(a1, a3), add_i(a1, a3)
    b4, b6, b5, b7 = add(a4, a6), sub(a4, a6), sub_i(a5, a7), add_i(a5, a7)
    c5 = ((b5[0] + b5[1]) * root, (b5[1] - b5[0]) * root)
    c7 = ((b7[1] - b7[0]) * root, (b7[0] + b7[1]) * -root)
    return [
        add(b0, b4), add(b1, c5), sub_i(b2, b6), add(b3, c7),
        sub(b0, b4), sub(b1, c5), add_i(b2, b6), sub(b3, c7),
    ]


def channelize_kernel(frames, volt_hbm, gain_hbm, taps_hbm, twist_hbm, table_hbm, out_ref,
                      volt_ref, gain_ref, taps_ref, twist_ref, table_ref,
                      part_ref, turn_ref, sorted_ref, sems):
    sources = (volt_hbm, taps_hbm, twist_hbm, gain_hbm, table_hbm)
    targets = (volt_ref, taps_ref, twist_ref, gain_ref, table_ref)
    copies = [pltpu.make_async_copy(s, t, sems.at[i]) for i, (s, t) in enumerate(zip(sources, targets))]
    for copy in copies:
        copy.start()
    antennas = volt_ref.shape[2]
    channels = volt_ref.shape[3]
    second = channels // FIRST
    spans = frames + TAPS - 1
    for copy in copies[0:3]:
        copy.wait()
    for g in range(spans):
        values = []
        for c in range(2):
            total = None
            for p in range(TAPS):
                f = g - (TAPS - 1) + p
                if 0 <= f < frames:
                    term = volt_ref[c, f].astype(jnp.float32) * taps_ref[p : p + 1, :]
                    total = term if total is None else total + term
            total = total.astype(jnp.bfloat16).astype(jnp.float32)
            values.append([total[:, j * second : (j + 1) * second] for j in range(FIRST)])
        for k, (re, im) in enumerate(eight_points(*values)):
            tw_re = twist_ref[0, k : k + 1, :]
            tw_im = twist_ref[1, k : k + 1, :]
            if k == 0:
                out_re, out_im = re, im
            else:
                out_re = re * tw_re - im * tw_im
                out_im = re * tw_im + im * tw_re
            row = (k * spans + g) * antennas
            part_ref[row : row + antennas, 0:second] = out_re.astype(jnp.bfloat16)
            part_ref[row : row + antennas, second:] = out_im.astype(jnp.bfloat16)
    copies[3].wait()
    both = jnp.concatenate([gain_ref[0], gain_ref[1]], axis=0)
    turn_ref[0:channels, 0 : 2 * antennas] = both.T
    copies[4].wait()
    blank = jnp.zeros(((2 * frames - spans) * antennas, second), jnp.float32)
    all_spectra = jnp.dot(part_ref[...], table_ref[...], preferred_element_type=jnp.float32)
    for k in range(FIRST):
        spectra = all_spectra[k * spans * antennas : (k + 1) * spans * antennas]
        gains = turn_ref[pl.ds(k, second, stride=FIRST), 0 : 2 * antennas].T
        gain_re = jnp.concatenate([gains[0:antennas]] * spans, axis=0)
        gain_im = jnp.concatenate([gains[antennas:]] * spans, axis=0)
        re, im = spectra[:, 0:second], spectra[:, second:]
        for c, volts in enumerate((re * gain_re - im * gain_im, re * gain_im + im * gain_re)):
            turned = jnp.concatenate([volts, blank], axis=0).T
            sorted_ref[pl.ds(2 * k + c, second, stride=OUT_PITCH), :] = turned
    width = 2 * FIRST
    for d in range(second):
        out_ref[d * width : (d + 1) * width] = sorted_ref[
            d * OUT_PITCH : d * OUT_PITCH + width].astype(jnp.bfloat16)


def footprint_kernel(cells_ref, offsets_ref, right_ref, left_ref):
    count = cells_ref.shape[1]
    rows, cols = cells_ref[0:1, :], cells_ref[1:2, :]
    share = (offsets_ref[...].astype(jnp.float32) + 0.5) * 0.125
    t_row, t_col = share[0:1, :], share[1:2, :]
    low = rows & (BAND - 1)
    place = (rows - low) * (GRID // BAND) + cols

    def table(height, first, weight):
        at = lax.broadcasted_iota(jnp.int32, (height, count), 0)
        near = jnp.where(at == first, 1.0 - weight, 0.0)
        return jnp.where(at == first + 1, weight, near).astype(jnp.bfloat16)

    right_ref[...] = table(BANDS * GRID, place, t_col)
    left_ref[...] = table(left_ref.shape[0], low, t_row)


def image_kernel(scale, x_ref, right_ref, left_ref, first_ref, second_ref, out_ref,
                 wide_ref, volt_ref, spread_ref, grid_ref, side_ref):
    blocks = 4
    frames = 4
    antennas = 16
    step = 4 * blocks
    for d in range(128):
        wide_ref[d * IN_PITCH : d * IN_PITCH + step] = x_ref[d * step : (d + 1) * step].astype(jnp.float32)
    for kk in range(2):
        for c in range(2):
            tail = None
            for t in range(blocks):
                turned = wide_ref[pl.ds(4 * t + 2 * kk + c, 128, stride=IN_PITCH), :].T
                own = turned[0 : frames * antennas]
                if tail is not None:
                    own = jnp.concatenate(
                        [own[0 : (TAPS - 1) * antennas] + tail, own[(TAPS - 1) * antennas :]], axis=0)
                tail = turned[frames * antennas : (frames + TAPS - 1) * antennas]
                for f in range(frames):
                    row = (kk * blocks + t) * frames + f
                    volt_ref[row // CHUNK, 2 * (row % CHUNK) + c] = own[f * antennas : (f + 1) * antennas]

    members = 2 * CHUNK

    def chunk(i, carry):
        for a in range(antennas):
            lanes = slice(a * 128, (a + 1) * 128)
            left = left_ref[0:BAND, lanes]
            for m in range(members):
                row = volt_ref[i, m, a : a + 1, :].astype(jnp.bfloat16)
                spread_ref[m * BAND : (m + 1) * BAND, lanes] = left * row
            edge = volt_ref[i, :, a, :].astype(jnp.bfloat16)
            spread_ref[members * BAND :, lanes] = edge * left_ref[BAND : BAND + 1, lanes]
        grid_ref[...] = lax.dot_general(
            spread_ref[...], right_ref[...], (((1,), (1,)), ((), ())),
            preferred_element_type=jnp.float32)
        for m in range(members):
            grid_ref[m * BAND : m * BAND + 1, GRID:] += grid_ref[
                members * BAND + m : members * BAND + m + 1, : (BANDS - 1) * GRID]
        for f in range(CHUNK):
            for c in range(2):
                m = 2 * f + c
                for h in range(BANDS):
                    side_ref[i * CHUNK + f, h * BAND : (h + 1) * BAND, c * GRID : (c + 1) * GRID] = grid_ref[
                        m * BAND : (m + 1) * BAND, h * GRID : (h + 1) * GRID].astype(jnp.bfloat16)
        return carry

    lax.fori_loop(0, 2 * blocks * frames // CHUNK, chunk, 0)
    for kk in range(2):
        total = None
        for t in range(0, blocks * frames, GROUP):
            first = kk * blocks * frames + t
            side = side_ref[first : first + GROUP].reshape(GROUP * GRID, 2 * GRID)
            half = jnp.dot(side, first_ref[...], preferred_element_type=jnp.float32).astype(jnp.bfloat16)
            mid = jnp.concatenate([
                jnp.concatenate([
                    half[f * GRID : (f + 1) * GRID, c * GRID : (c + 1) * GRID] for f in range(GROUP)], axis=1)
                for c in range(2)], axis=0)
            sky = jnp.dot(second_ref[...], mid, preferred_element_type=jnp.float32)
            power = sky[0:GRID] * sky[0:GRID] + sky[GRID:] * sky[GRID:]
            for f in range(GROUP):
                part = power[:, f * GRID : (f + 1) * GRID]
                total = part if total is None else total + part
        out_ref[kk] = total * scale


def local(voltages, calibrated_gain, cells, offsets):
    _, frames, antennas, channels = voltages.shape
    second = channels // FIRST
    devices = lax.axis_size("chan") * lax.axis_size("tblk")
    all_antennas = antennas * lax.axis_size("chan")
    scale = 1.0 / (all_antennas * channels * frames * lax.axis_size("tblk"))
    rows = channels * 2

    send = pl.pallas_call(
        lambda *refs: channelize_kernel(frames, *refs),
        out_shape=jax.ShapeDtypeStruct((rows, second), jnp.bfloat16),
        in_specs=[pl.BlockSpec(memory_space=pl.ANY)] * 5,
        scratch_shapes=[
            pltpu.VMEM(voltages.shape, jnp.bfloat16),
            pltpu.VMEM(calibrated_gain.shape, jnp.float32),
            pltpu.VMEM((TAPS, channels), jnp.float32),
            pltpu.VMEM((2, FIRST, second), jnp.float32),
            pltpu.VMEM((2 * second, 2 * second), jnp.bfloat16),
            pltpu.VMEM((FIRST * (frames + TAPS - 1) * antennas, 2 * second), jnp.bfloat16),
            pltpu.VMEM((channels + FIRST, 128), jnp.float32),
            pltpu.VMEM((second * OUT_PITCH + 2 * FIRST, second), jnp.float32),
            pltpu.SemaphoreType.DMA((5,)),
        ],
        compiler_params=pltpu.CompilerParams(vmem_limit_bytes=60 * 1024 * 1024),
        name="channelize",
    )(
        voltages, calibrated_gain, jnp.asarray(prototype(channels)),
        jnp.asarray(twiddle(channels)), jnp.asarray(dft_right(second)),
    )

    def by_member(table):
        return table.reshape(2, all_antennas // antennas, antennas).transpose(0, 2, 1).reshape(2, all_antennas)

    right, left = pl.pallas_call(
        footprint_kernel,
        out_shape=(
            jax.ShapeDtypeStruct((BANDS * GRID, all_antennas), jnp.bfloat16),
            jax.ShapeDtypeStruct((BAND + 16, all_antennas), jnp.bfloat16),
        ),
        compiler_params=pltpu.CompilerParams(vmem_limit_bytes=VMEM_BYTES),
        cost_estimate=pl.CostEstimate(flops=10_000_000, bytes_accessed=1_500_000, transcendentals=0),
        name="footprint",
    )(by_member(cells), by_member(offsets))

    send = send.reshape(devices, rows // devices, second)
    received = lax.all_to_all(send, ("chan", "tblk"), split_axis=0, concat_axis=0, tiled=True)
    received = received.reshape(rows, second)

    members = 2 * CHUNK
    chunks = 2 * frames * lax.axis_size("tblk") // CHUNK
    return pl.pallas_call(
        lambda *refs: image_kernel(scale, *refs),
        out_shape=jax.ShapeDtypeStruct((2, GRID, GRID), jnp.float32),
        scratch_shapes=[
            pltpu.VMEM((128 * IN_PITCH + 16, second), jnp.float32),
            pltpu.VMEM((chunks, members, antennas, 128), jnp.float32),
            pltpu.VMEM((members * (BAND + 1), all_antennas), jnp.bfloat16),
            pltpu.VMEM((members * (BAND + 1), BANDS * GRID), jnp.float32),
            pltpu.VMEM((chunks * CHUNK, GRID, 2 * GRID), jnp.bfloat16),
        ],
        compiler_params=pltpu.CompilerParams(vmem_limit_bytes=VMEM_BYTES),
        name="image",
    )(received, right, left, jnp.asarray(dft_right(GRID)), jnp.asarray(dft_left(GRID)))


def solution(mesh):
    placed = (P(None, "tblk", "chan", None), P(None, "chan", None), P(), P())
    return jax.shard_map(
        local,
        mesh=mesh,
        in_specs=placed,
        out_specs=P(("chan", "tblk"), None, None),
        check_vma=False,
    )
```

```python
import math

import jax
import jax.numpy as jnp
import numpy as np
from jax import lax
from jax.experimental import pallas as pl
from jax.experimental.pallas import tpu as pltpu
from jax.sharding import PartitionSpec as P

GRID = 128
TAPS = 4
FIRST = 8
BANDS = 4
BAND = GRID // BANDS
PARTS = 2
IN_PITCH = 17
GROUP = 16
CHUNK = 16
VMEM_BYTES = 32 * 1024 * 1024


def prototype(channels):
    span = TAPS * channels
    places = np.arange(span, dtype=np.float64) + 0.5
    window = 0.54 - 0.46 * np.cos(places * (2.0 * math.pi / span))
    return (np.sinc((places - 0.5 * span) / channels) * window).reshape(TAPS, channels).astype(np.float32)


def twiddle(channels):
    second = channels // FIRST
    phases = (np.arange(FIRST)[:, None] * np.arange(second)[None, :] % channels) * (2.0 * math.pi / channels)
    return np.stack([np.cos(phases), -np.sin(phases)]).astype(np.float32)


def dft_parts(length):
    points = np.arange(length)
    phases = (points[:, None] * points[None, :] % length) * (2.0 * math.pi / length)
    return np.cos(phases), np.sin(phases)


def dft_right(length):
    cosine, sine = dft_parts(length)
    return np.block([[cosine, -sine], [sine, cosine]]).astype(jnp.bfloat16)


def dft_left(length):
    cosine, sine = dft_parts(length)
    return np.block([[cosine, sine], [-sine, cosine]]).astype(jnp.bfloat16)


def eight_points(re, im):
    add = lambda p, q: (p[0] + q[0], p[1] + q[1])
    sub = lambda p, q: (p[0] - q[0], p[1] - q[1])
    sub_i = lambda p, q: (p[0] + q[1], p[1] - q[0])
    add_i = lambda p, q: (p[0] - q[1], p[1] + q[0])
    root = math.sqrt(0.5)
    w = list(zip(re, im))
    a0, a1, a2, a3 = add(w[0], w[4]), sub(w[0], w[4]), add(w[2], w[6]), sub(w[2], w[6])
    a4, a5, a6, a7 = add(w[1], w[5]), sub(w[1], w[5]), add(w[3], w[7]), sub(w[3], w[7])
    b0, b2, b1, b3 = add(a0, a2), sub(a0, a2), sub_i(a1, a3), add_i(a1, a3)
    b4, b6, b5, b7 = add(a4, a6), sub(a4, a6), sub_i(a5, a7), add_i(a5, a7)
    c5 = ((b5[0] + b5[1]) * root, (b5[1] - b5[0]) * root)
    c7 = ((b7[1] - b7[0]) * root, (b7[0] + b7[1]) * -root)
    return [
        add(b0, b4), add(b1, c5), sub_i(b2, b6), add(b3, c7),
        sub(b0, b4), sub(b1, c5), add_i(b2, b6), sub(b3, c7),
    ]


def channelize_kernel(frames, volt_hbm, gain_hbm, taps_hbm, twist_hbm, table_hbm, out_ref,
                      volt_ref, gain_ref, taps_ref, twist_ref, table_ref,
                      part_ref, turn_ref, sorted_ref, pack_ref, sems):
    sources = (volt_hbm, taps_hbm, twist_hbm, gain_hbm, table_hbm)
    targets = (volt_ref, taps_ref, twist_ref, gain_ref, table_ref)
    copies = [pltpu.make_async_copy(s, t, sems.at[i]) for i, (s, t) in enumerate(zip(sources, targets))]
    for copy in copies:
        copy.start()
    antennas = volt_ref.shape[2]
    channels = volt_ref.shape[3]
    second = channels // FIRST
    spans = frames + TAPS - 1
    for copy in copies[0:3]:
        copy.wait()
    for g in range(spans):
        values = []
        for c in range(2):
            total = None
            for p in range(TAPS):
                f = g - (TAPS - 1) + p
                if 0 <= f < frames:
                    term = volt_ref[c, f].astype(jnp.float32) * taps_ref[p : p + 1, :]
                    total = term if total is None else total + term
            total = total.astype(jnp.bfloat16).astype(jnp.float32)
            values.append([total[:, j * second : (j + 1) * second] for j in range(FIRST)])
        for k, (re, im) in enumerate(eight_points(*values)):
            tw_re = twist_ref[0, k : k + 1, :]
            tw_im = twist_ref[1, k : k + 1, :]
            if k == 0:
                out_re, out_im = re, im
            else:
                out_re = re * tw_re - im * tw_im
                out_im = re * tw_im + im * tw_re
            row = (k * spans + g) * antennas
            part_ref[row : row + antennas, 0:second] = out_re.astype(jnp.bfloat16)
            part_ref[row : row + antennas, second:] = out_im.astype(jnp.bfloat16)
    copies[3].wait()
    both = jnp.concatenate([gain_ref[0], gain_ref[1]], axis=0)
    turn_ref[0:channels, 0 : 2 * antennas] = both.T
    copies[4].wait()
    blank = jnp.zeros(((2 * frames - spans) * antennas, second), jnp.float32)
    share = FIRST // PARTS
    lines = spans * antennas
    sends = []
    for h in range(PARTS):
        all_spectra = jnp.dot(
            part_ref[h * share * lines : (h + 1) * share * lines], table_ref[...],
            preferred_element_type=jnp.float32)
        for q in range(share):
            k = h * share + q
            spectra = all_spectra[q * lines : (q + 1) * lines]
            gains = turn_ref[pl.ds(k, second, stride=FIRST), 0 : 2 * antennas].T
            gain_re = jnp.concatenate([gains[0:antennas]] * spans, axis=0)
            gain_im = jnp.concatenate([gains[antennas:]] * spans, axis=0)
            re, im = spectra[:, 0:second], spectra[:, second:]
            for c, volts in enumerate((re * gain_re - im * gain_im, re * gain_im + im * gain_re)):
                turned = jnp.concatenate([volts, blank], axis=0).T
                sorted_ref[h, pl.ds(2 * q + c, second, stride=2 * share), :] = turned
        width = 2 * share
        pack_ref[:, h] = sorted_ref[h, 0 : second * width].reshape(second, width, second).astype(jnp.bfloat16)
        sends.append(pltpu.make_async_copy(pack_ref.at[:, h], out_ref.at[:, h], sems.at[len(copies) + h]))
        sends[-1].start()
    for send in sends:
        send.wait()


def footprint_kernel(cells_ref, offsets_ref, right_ref, left_ref):
    count = cells_ref.shape[1]
    rows, cols = cells_ref[0:1, :], cells_ref[1:2, :]
    share = (offsets_ref[...].astype(jnp.float32) + 0.5) * 0.125
    t_row, t_col = share[0:1, :], share[1:2, :]
    low = rows & (BAND - 1)
    place = (rows - low) * (GRID // BAND) + cols

    def table(height, first, weight):
        at = lax.broadcasted_iota(jnp.int32, (height, count), 0)
        near = jnp.where(at == first, 1.0 - weight, 0.0)
        return jnp.where(at == first + 1, weight, near).astype(jnp.bfloat16)

    right_ref[...] = table(BANDS * GRID, place, t_col)
    left_ref[...] = table(left_ref.shape[0], low, t_row)


def image_kernel(scale, x_ref, right_ref, left_ref, first_ref, second_ref, out_ref,
                 wide_ref, volt_ref, spread_ref, grid_ref, side_ref):
    blocks = 4
    frames = 4
    antennas = 16
    step = 4 * blocks
    for d in range(128):
        wide_ref[d * IN_PITCH : d * IN_PITCH + step] = x_ref[d * step : (d + 1) * step].astype(jnp.float32)
    for kk in range(2):
        for c in range(2):
            tail = None
            for t in range(blocks):
                turned = wide_ref[pl.ds(4 * t + 2 * kk + c, 128, stride=IN_PITCH), :].T
                own = turned[0 : frames * antennas]
                if tail is not None:
                    own = jnp.concatenate(
                        [own[0 : (TAPS - 1) * antennas] + tail, own[(TAPS - 1) * antennas :]], axis=0)
                tail = turned[frames * antennas : (frames + TAPS - 1) * antennas]
                for f in range(frames):
                    row = (kk * blocks + t) * frames + f
                    volt_ref[row // CHUNK, 2 * (row % CHUNK) + c] = own[f * antennas : (f + 1) * antennas]

    members = 2 * CHUNK

    def chunk(i, carry):
        for a in range(antennas):
            lanes = slice(a * 128, (a + 1) * 128)
            left = left_ref[0:BAND, lanes]
            for m in range(members):
                row = volt_ref[i, m, a : a + 1, :].astype(jnp.bfloat16)
                spread_ref[m * BAND : (m + 1) * BAND, lanes] = left * row
            edge = volt_ref[i, :, a, :].astype(jnp.bfloat16)
            spread_ref[members * BAND :, lanes] = edge * left_ref[BAND : BAND + 1, lanes]
        grid_ref[...] = lax.dot_general(
            spread_ref[...], right_ref[...], (((1,), (1,)), ((), ())),
            preferred_element_type=jnp.float32)
        for m in range(members):
            grid_ref[m * BAND : m * BAND + 1, GRID:] += grid_ref[
                members * BAND + m : members * BAND + m + 1, : (BANDS - 1) * GRID]
        for f in range(CHUNK):
            for c in range(2):
                m = 2 * f + c
                for h in range(BANDS):
                    side_ref[i * CHUNK + f, h * BAND : (h + 1) * BAND, c * GRID : (c + 1) * GRID] = grid_ref[
                        m * BAND : (m + 1) * BAND, h * GRID : (h + 1) * GRID].astype(jnp.bfloat16)
        return carry

    lax.fori_loop(0, 2 * blocks * frames // CHUNK, chunk, 0)
    for kk in range(2):
        total = None
        for t in range(0, blocks * frames, GROUP):
            first = kk * blocks * frames + t
            side = side_ref[first : first + GROUP].reshape(GROUP * GRID, 2 * GRID)
            half = jnp.dot(side, first_ref[...], preferred_element_type=jnp.float32).astype(jnp.bfloat16)
            mid = jnp.concatenate([
                jnp.concatenate([
                    half[f * GRID : (f + 1) * GRID, c * GRID : (c + 1) * GRID] for f in range(GROUP)], axis=1)
                for c in range(2)], axis=0)
            sky = jnp.dot(second_ref[...], mid, preferred_element_type=jnp.float32)
            power = sky[0:GRID] * sky[0:GRID] + sky[GRID:] * sky[GRID:]
            for f in range(GROUP):
                part = power[:, f * GRID : (f + 1) * GRID]
                total = part if total is None else total + part
        out_ref[kk] = total * scale


def local(voltages, calibrated_gain, cells, offsets):
    _, frames, antennas, channels = voltages.shape
    second = channels // FIRST
    devices = lax.axis_size("chan") * lax.axis_size("tblk")
    all_antennas = antennas * lax.axis_size("chan")
    scale = 1.0 / (all_antennas * channels * frames * lax.axis_size("tblk"))
    rows = channels * 2

    send = pl.pallas_call(
        lambda *refs: channelize_kernel(frames, *refs),
        out_shape=jax.ShapeDtypeStruct((second, PARTS, rows // second // PARTS, second), jnp.bfloat16),
        out_specs=pl.BlockSpec(memory_space=pl.ANY),
        in_specs=[pl.BlockSpec(memory_space=pl.ANY)] * 5,
        scratch_shapes=[
            pltpu.VMEM(voltages.shape, jnp.bfloat16),
            pltpu.VMEM(calibrated_gain.shape, jnp.float32),
            pltpu.VMEM((TAPS, channels), jnp.float32),
            pltpu.VMEM((2, FIRST, second), jnp.float32),
            pltpu.VMEM((2 * second, 2 * second), jnp.bfloat16),
            pltpu.VMEM((FIRST * (frames + TAPS - 1) * antennas, 2 * second), jnp.bfloat16),
            pltpu.VMEM((channels + FIRST, 128), jnp.float32),
            pltpu.VMEM((PARTS, rows // PARTS + FIRST, second), jnp.float32),
            pltpu.VMEM((second, PARTS, rows // second // PARTS, second), jnp.bfloat16),
            pltpu.SemaphoreType.DMA((5 + PARTS,)),
        ],
        compiler_params=pltpu.CompilerParams(vmem_limit_bytes=60 * 1024 * 1024),
        name="channelize",
    )(
        voltages, calibrated_gain, jnp.asarray(prototype(channels)),
        jnp.asarray(twiddle(channels)), jnp.asarray(dft_right(second)),
    )

    def by_member(table):
        return table.reshape(2, all_antennas // antennas, antennas).transpose(0, 2, 1).reshape(2, all_antennas)

    right, left = pl.pallas_call(
        footprint_kernel,
        out_shape=(
            jax.ShapeDtypeStruct((BANDS * GRID, all_antennas), jnp.bfloat16),
            jax.ShapeDtypeStruct((BAND + 16, all_antennas), jnp.bfloat16),
        ),
        compiler_params=pltpu.CompilerParams(vmem_limit_bytes=VMEM_BYTES),
        cost_estimate=pl.CostEstimate(flops=10_000_000, bytes_accessed=1_500_000, transcendentals=0),
        name="footprint",
    )(by_member(cells), by_member(offsets))

    send = send.reshape(devices, rows // devices, second)
    received = lax.all_to_all(send, ("chan", "tblk"), split_axis=0, concat_axis=0, tiled=True)
    received = received.reshape(rows, second)

    members = 2 * CHUNK
    chunks = 2 * frames * lax.axis_size("tblk") // CHUNK
    return pl.pallas_call(
        lambda *refs: image_kernel(scale, *refs),
        out_shape=jax.ShapeDtypeStruct((2, GRID, GRID), jnp.float32),
        scratch_shapes=[
            pltpu.VMEM((128 * IN_PITCH + 16, second), jnp.float32),
            pltpu.VMEM((chunks, members, antennas, 128), jnp.float32),
            pltpu.VMEM((members * (BAND + 1), all_antennas), jnp.bfloat16),
            pltpu.VMEM((members * (BAND + 1), BANDS * GRID), jnp.float32),
            pltpu.VMEM((chunks * CHUNK, GRID, 2 * GRID), jnp.bfloat16),
        ],
        compiler_params=pltpu.CompilerParams(vmem_limit_bytes=VMEM_BYTES),
        name="image",
    )(received, right, left, jnp.asarray(dft_right(GRID)), jnp.asarray(dft_left(GRID)))


def solution(mesh):
    placed = (P(None, "tblk", "chan", None), P(None, "chan", None), P(), P())
    return jax.shard_map(
        local,
        mesh=mesh,
        in_specs=placed,
        out_specs=P(("chan", "tblk"), None, None),
        check_vma=False,
    )
```

```python
import math

import jax
import jax.numpy as jnp
import numpy as np
from jax import lax
from jax.experimental import pallas as pl
from jax.experimental.pallas import tpu as pltpu
from jax.sharding import PartitionSpec as P

GRID = 128
TAPS = 4
FIRST = 8
BANDS = 4
BAND = GRID // BANDS
PARTS = 2
IN_PITCH = 17
GROUP = 8
CHUNK = 16
VMEM_BYTES = 32 * 1024 * 1024


def prototype(channels):
    span = TAPS * channels
    places = np.arange(span, dtype=np.float64) + 0.5
    window = 0.54 - 0.46 * np.cos(places * (2.0 * math.pi / span))
    return (np.sinc((places - 0.5 * span) / channels) * window).reshape(TAPS, channels).astype(np.float32)


def twiddle(channels):
    second = channels // FIRST
    phases = (np.arange(FIRST)[:, None] * np.arange(second)[None, :] % channels) * (2.0 * math.pi / channels)
    return np.stack([np.cos(phases), -np.sin(phases)]).astype(np.float32)


def dft_parts(length):
    points = np.arange(length)
    phases = (points[:, None] * points[None, :] % length) * (2.0 * math.pi / length)
    return np.cos(phases), np.sin(phases)


def dft_right(length):
    cosine, sine = dft_parts(length)
    return np.block([[cosine, -sine], [sine, cosine]]).astype(jnp.bfloat16)


def dft_left(length):
    cosine, sine = dft_parts(length)
    return np.block([[cosine, sine], [-sine, cosine]]).astype(jnp.bfloat16)


def eight_points(re, im):
    add = lambda p, q: (p[0] + q[0], p[1] + q[1])
    sub = lambda p, q: (p[0] - q[0], p[1] - q[1])
    sub_i = lambda p, q: (p[0] + q[1], p[1] - q[0])
    add_i = lambda p, q: (p[0] - q[1], p[1] + q[0])
    root = math.sqrt(0.5)
    w = list(zip(re, im))
    a0, a1, a2, a3 = add(w[0], w[4]), sub(w[0], w[4]), add(w[2], w[6]), sub(w[2], w[6])
    a4, a5, a6, a7 = add(w[1], w[5]), sub(w[1], w[5]), add(w[3], w[7]), sub(w[3], w[7])
    b0, b2, b1, b3 = add(a0, a2), sub(a0, a2), sub_i(a1, a3), add_i(a1, a3)
    b4, b6, b5, b7 = add(a4, a6), sub(a4, a6), sub_i(a5, a7), add_i(a5, a7)
    c5 = ((b5[0] + b5[1]) * root, (b5[1] - b5[0]) * root)
    c7 = ((b7[1] - b7[0]) * root, (b7[0] + b7[1]) * -root)
    return [
        add(b0, b4), add(b1, c5), sub_i(b2, b6), add(b3, c7),
        sub(b0, b4), sub(b1, c5), add_i(b2, b6), sub(b3, c7),
    ]


def channelize_kernel(frames, volt_hbm, gain_hbm, taps_hbm, twist_hbm, table_hbm, out_ref,
                      volt_ref, gain_ref, taps_ref, twist_ref, table_ref,
                      part_ref, turn_ref, sorted_ref, pack_ref, sems):
    sources = (volt_hbm, taps_hbm, twist_hbm, gain_hbm, table_hbm)
    targets = (volt_ref, taps_ref, twist_ref, gain_ref, table_ref)
    copies = [pltpu.make_async_copy(s, t, sems.at[i]) for i, (s, t) in enumerate(zip(sources, targets))]
    for copy in copies:
        copy.start()
    antennas = volt_ref.shape[2]
    channels = volt_ref.shape[3]
    second = channels // FIRST
    spans = frames + TAPS - 1
    for copy in copies[0:3]:
        copy.wait()
    for g in range(spans):
        values = []
        for c in range(2):
            total = None
            for p in range(TAPS):
                f = g - (TAPS - 1) + p
                if 0 <= f < frames:
                    term = volt_ref[c, f].astype(jnp.float32) * taps_ref[p : p + 1, :]
                    total = term if total is None else total + term
            total = total.astype(jnp.bfloat16).astype(jnp.float32)
            values.append([total[:, j * second : (j + 1) * second] for j in range(FIRST)])
        for k, (re, im) in enumerate(eight_points(*values)):
            tw_re = twist_ref[0, k : k + 1, :]
            tw_im = twist_ref[1, k : k + 1, :]
            if k == 0:
                out_re, out_im = re, im
            else:
                out_re = re * tw_re - im * tw_im
                out_im = re * tw_im + im * tw_re
            row = (k * spans + g) * antennas
            part_ref[row : row + antennas, 0:second] = out_re.astype(jnp.bfloat16)
            part_ref[row : row + antennas, second:] = out_im.astype(jnp.bfloat16)
    copies[3].wait()
    both = jnp.concatenate([gain_ref[0], gain_ref[1]], axis=0)
    turn_ref[0:channels, 0 : 2 * antennas] = both.T
    copies[4].wait()
    blank = jnp.zeros(((2 * frames - spans) * antennas, second), jnp.float32)
    share = FIRST // PARTS
    lines = spans * antennas
    sends = []
    for h in range(PARTS):
        all_spectra = jnp.dot(
            part_ref[h * share * lines : (h + 1) * share * lines], table_ref[...],
            preferred_element_type=jnp.float32)
        for q in range(share):
            k = h * share + q
            spectra = all_spectra[q * lines : (q + 1) * lines]
            gains = turn_ref[pl.ds(k, second, stride=FIRST), 0 : 2 * antennas].T
            gain_re = jnp.concatenate([gains[0:antennas]] * spans, axis=0)
            gain_im = jnp.concatenate([gains[antennas:]] * spans, axis=0)
            re, im = spectra[:, 0:second], spectra[:, second:]
            for c, volts in enumerate((re * gain_re - im * gain_im, re * gain_im + im * gain_re)):
                turned = jnp.concatenate([volts, blank], axis=0).T
                sorted_ref[h, pl.ds(2 * q + c, second, stride=2 * share), :] = turned
        width = 2 * share
        pack_ref[:, h] = sorted_ref[h, 0 : second * width].reshape(second, width, second).astype(jnp.bfloat16)
        sends.append(pltpu.make_async_copy(pack_ref.at[:, h], out_ref.at[:, h], sems.at[len(copies) + h]))
        sends[-1].start()
    for send in sends:
        send.wait()


def footprint_kernel(cells_ref, offsets_ref, right_ref, left_ref):
    count = cells_ref.shape[1]
    rows, cols = cells_ref[0:1, :], cells_ref[1:2, :]
    share = (offsets_ref[...].astype(jnp.float32) + 0.5) * 0.125
    t_row, t_col = share[0:1, :], share[1:2, :]
    low = rows & (BAND - 1)
    place = (rows - low) * (GRID // BAND) + cols

    def table(height, first, weight):
        at = lax.broadcasted_iota(jnp.int32, (height, count), 0)
        near = jnp.where(at == first, 1.0 - weight, 0.0)
        return jnp.where(at == first + 1, weight, near).astype(jnp.bfloat16)

    right_ref[...] = table(BANDS * GRID, place, t_col)
    left_ref[...] = table(left_ref.shape[0], low, t_row)


def image_kernel(scale, x_ref, right_ref, left_ref, first_ref, second_ref, out_ref,
                 wide_ref, volt_ref, spread_ref, grid_ref, side_ref):
    blocks = 4
    frames = 4
    antennas = 16
    step = 4 * blocks
    for d in range(128):
        wide_ref[d * IN_PITCH : d * IN_PITCH + step] = x_ref[d * step : (d + 1) * step].astype(jnp.float32)
    for kk in range(2):
        for c in range(2):
            tail = None
            for t in range(blocks):
                turned = wide_ref[pl.ds(4 * t + 2 * kk + c, 128, stride=IN_PITCH), :].T
                own = turned[0 : frames * antennas]
                if tail is not None:
                    own = jnp.concatenate(
                        [own[0 : (TAPS - 1) * antennas] + tail, own[(TAPS - 1) * antennas :]], axis=0)
                tail = turned[frames * antennas : (frames + TAPS - 1) * antennas]
                for f in range(frames):
                    row = (kk * blocks + t) * frames + f
                    volt_ref[row // CHUNK, 2 * (row % CHUNK) + c] = own[f * antennas : (f + 1) * antennas]

    members = 2 * CHUNK

    def chunk(i, carry):
        for a in range(antennas):
            lanes = slice(a * 128, (a + 1) * 128)
            left = left_ref[0:BAND, lanes]
            for m in range(members):
                row = volt_ref[i, m, a : a + 1, :].astype(jnp.bfloat16)
                spread_ref[m * BAND : (m + 1) * BAND, lanes] = left * row
            edge = volt_ref[i, :, a, :].astype(jnp.bfloat16)
            spread_ref[members * BAND :, lanes] = edge * left_ref[BAND : BAND + 1, lanes]
        grid_ref[...] = lax.dot_general(
            spread_ref[...], right_ref[...], (((1,), (1,)), ((), ())),
            preferred_element_type=jnp.float32)
        for m in range(members):
            grid_ref[m * BAND : m * BAND + 1, GRID:] += grid_ref[
                members * BAND + m : members * BAND + m + 1, : (BANDS - 1) * GRID]
        for f in range(CHUNK):
            for c in range(2):
                m = 2 * f + c
                for h in range(BANDS):
                    side_ref[i * CHUNK + f, h * BAND : (h + 1) * BAND, c * GRID : (c + 1) * GRID] = grid_ref[
                        m * BAND : (m + 1) * BAND, h * GRID : (h + 1) * GRID].astype(jnp.bfloat16)
        return carry

    lax.fori_loop(0, 2 * blocks * frames // CHUNK, chunk, 0)
    for kk in range(2):
        total = None
        for t in range(0, blocks * frames, GROUP):
            first = kk * blocks * frames + t
            side = side_ref[first : first + GROUP].reshape(GROUP * GRID, 2 * GRID)
            half = jnp.dot(side, first_ref[...], preferred_element_type=jnp.float32).astype(jnp.bfloat16)
            mid = jnp.concatenate([
                jnp.concatenate([
                    half[f * GRID : (f + 1) * GRID, c * GRID : (c + 1) * GRID] for f in range(GROUP)], axis=1)
                for c in range(2)], axis=0)
            sky = jnp.dot(second_ref[...], mid, preferred_element_type=jnp.float32)
            power = sky[0:GRID] * sky[0:GRID] + sky[GRID:] * sky[GRID:]
            for f in range(GROUP):
                part = power[:, f * GRID : (f + 1) * GRID]
                total = part if total is None else total + part
        out_ref[kk] = total * scale


def local(voltages, calibrated_gain, cells, offsets):
    _, frames, antennas, channels = voltages.shape
    second = channels // FIRST
    devices = lax.axis_size("chan") * lax.axis_size("tblk")
    all_antennas = antennas * lax.axis_size("chan")
    scale = 1.0 / (all_antennas * channels * frames * lax.axis_size("tblk"))
    rows = channels * 2

    send = pl.pallas_call(
        lambda *refs: channelize_kernel(frames, *refs),
        out_shape=jax.ShapeDtypeStruct((second, PARTS, rows // second // PARTS, second), jnp.bfloat16),
        out_specs=pl.BlockSpec(memory_space=pl.ANY),
        in_specs=[pl.BlockSpec(memory_space=pl.ANY)] * 5,
        scratch_shapes=[
            pltpu.VMEM(voltages.shape, jnp.bfloat16),
            pltpu.VMEM(calibrated_gain.shape, jnp.float32),
            pltpu.VMEM((TAPS, channels), jnp.float32),
            pltpu.VMEM((2, FIRST, second), jnp.float32),
            pltpu.VMEM((2 * second, 2 * second), jnp.bfloat16),
            pltpu.VMEM((FIRST * (frames + TAPS - 1) * antennas, 2 * second), jnp.bfloat16),
            pltpu.VMEM((channels + FIRST, 128), jnp.float32),
            pltpu.VMEM((PARTS, rows // PARTS + FIRST, second), jnp.float32),
            pltpu.VMEM((second, PARTS, rows // second // PARTS, second), jnp.bfloat16),
            pltpu.SemaphoreType.DMA((5 + PARTS,)),
        ],
        compiler_params=pltpu.CompilerParams(vmem_limit_bytes=60 * 1024 * 1024),
        name="channelize",
    )(
        voltages, calibrated_gain, jnp.asarray(prototype(channels)),
        jnp.asarray(twiddle(channels)), jnp.asarray(dft_right(second)),
    )

    def by_member(table):
        return table.reshape(2, all_antennas // antennas, antennas).transpose(0, 2, 1).reshape(2, all_antennas)

    right, left = pl.pallas_call(
        footprint_kernel,
        out_shape=(
            jax.ShapeDtypeStruct((BANDS * GRID, all_antennas), jnp.bfloat16),
            jax.ShapeDtypeStruct((BAND + 16, all_antennas), jnp.bfloat16),
        ),
        compiler_params=pltpu.CompilerParams(vmem_limit_bytes=VMEM_BYTES),
        cost_estimate=pl.CostEstimate(flops=10_000_000, bytes_accessed=1_500_000, transcendentals=0),
        name="footprint",
    )(by_member(cells), by_member(offsets))

    send = send.reshape(devices, rows // devices, second)
    received = lax.all_to_all(send, ("chan", "tblk"), split_axis=0, concat_axis=0, tiled=True)
    received = received.reshape(rows, second)

    members = 2 * CHUNK
    chunks = 2 * frames * lax.axis_size("tblk") // CHUNK
    return pl.pallas_call(
        lambda *refs: image_kernel(scale, *refs),
        out_shape=jax.ShapeDtypeStruct((2, GRID, GRID), jnp.float32),
        scratch_shapes=[
            pltpu.VMEM((128 * IN_PITCH + 16, second), jnp.float32),
            pltpu.VMEM((chunks, members, antennas, 128), jnp.float32),
            pltpu.VMEM((members * (BAND + 1), all_antennas), jnp.bfloat16),
            pltpu.VMEM((members * (BAND + 1), BANDS * GRID), jnp.float32),
            pltpu.VMEM((chunks * CHUNK, GRID, 2 * GRID), jnp.bfloat16),
        ],
        compiler_params=pltpu.CompilerParams(vmem_limit_bytes=VMEM_BYTES),
        name="image",
    )(received, right, left, jnp.asarray(dft_right(GRID)), jnp.asarray(dft_left(GRID)))


def solution(mesh):
    placed = (P(None, "tblk", "chan", None), P(None, "chan", None), P(), P())
    return jax.shard_map(
        local,
        mesh=mesh,
        in_specs=placed,
        out_specs=P(("chan", "tblk"), None, None),
        check_vma=False,
    )
```

```python
import math

import jax
import jax.numpy as jnp
import numpy as np
from jax import lax
from jax.experimental import pallas as pl
from jax.experimental.pallas import tpu as pltpu
from jax.sharding import PartitionSpec as P

GRID = 128
TAPS = 4
FIRST = 8
BANDS = 4
BAND = GRID // BANDS
PARTS = 2
IN_PITCH = 17
GROUP = 8
CHUNK = 16
VMEM_BYTES = 32 * 1024 * 1024


def prototype(channels):
    span = TAPS * channels
    places = np.arange(span, dtype=np.float64) + 0.5
    window = 0.54 - 0.46 * np.cos(places * (2.0 * math.pi / span))
    return (np.sinc((places - 0.5 * span) / channels) * window).reshape(TAPS, channels).astype(np.float32)


def twiddle(channels):
    second = channels // FIRST
    phases = (np.arange(FIRST)[:, None] * np.arange(second)[None, :] % channels) * (2.0 * math.pi / channels)
    return np.stack([np.cos(phases), -np.sin(phases)]).astype(np.float32)


def dft_parts(length):
    points = np.arange(length)
    phases = (points[:, None] * points[None, :] % length) * (2.0 * math.pi / length)
    return np.cos(phases), np.sin(phases)


def dft_right(length):
    cosine, sine = dft_parts(length)
    return np.block([[cosine, -sine], [sine, cosine]]).astype(jnp.bfloat16)


def dft_left(length):
    cosine, sine = dft_parts(length)
    return np.block([[cosine, sine], [-sine, cosine]]).astype(jnp.bfloat16)


def eight_points(re, im):
    add = lambda p, q: (p[0] + q[0], p[1] + q[1])
    sub = lambda p, q: (p[0] - q[0], p[1] - q[1])
    sub_i = lambda p, q: (p[0] + q[1], p[1] - q[0])
    add_i = lambda p, q: (p[0] - q[1], p[1] + q[0])
    root = math.sqrt(0.5)
    w = list(zip(re, im))
    a0, a1, a2, a3 = add(w[0], w[4]), sub(w[0], w[4]), add(w[2], w[6]), sub(w[2], w[6])
    a4, a5, a6, a7 = add(w[1], w[5]), sub(w[1], w[5]), add(w[3], w[7]), sub(w[3], w[7])
    b0, b2, b1, b3 = add(a0, a2), sub(a0, a2), sub_i(a1, a3), add_i(a1, a3)
    b4, b6, b5, b7 = add(a4, a6), sub(a4, a6), sub_i(a5, a7), add_i(a5, a7)
    c5 = ((b5[0] + b5[1]) * root, (b5[1] - b5[0]) * root)
    c7 = ((b7[1] - b7[0]) * root, (b7[0] + b7[1]) * -root)
    return [
        add(b0, b4), add(b1, c5), sub_i(b2, b6), add(b3, c7),
        sub(b0, b4), sub(b1, c5), add_i(b2, b6), sub(b3, c7),
    ]


def channelize_kernel(frames, volt_hbm, gain_hbm, taps_hbm, twist_hbm, table_hbm, out_ref,
                      volt_ref, gain_ref, taps_ref, twist_ref, table_ref,
                      part_ref, turn_ref, sorted_ref, pack_ref, sems):
    sources = (volt_hbm, taps_hbm, twist_hbm, gain_hbm, table_hbm)
    targets = (volt_ref, taps_ref, twist_ref, gain_ref, table_ref)
    copies = [pltpu.make_async_copy(s, t, sems.at[i]) for i, (s, t) in enumerate(zip(sources, targets))]
    for copy in copies:
        copy.start()
    antennas = volt_ref.shape[2]
    channels = volt_ref.shape[3]
    second = channels // FIRST
    spans = frames + TAPS - 1
    for copy in copies[0:3]:
        copy.wait()
    for g in range(spans):
        values = []
        for c in range(2):
            total = None
            for p in range(TAPS):
                f = g - (TAPS - 1) + p
                if 0 <= f < frames:
                    term = volt_ref[c, f].astype(jnp.float32) * taps_ref[p : p + 1, :]
                    total = term if total is None else total + term
            total = total.astype(jnp.bfloat16).astype(jnp.float32)
            values.append([total[:, j * second : (j + 1) * second] for j in range(FIRST)])
        for k, (re, im) in enumerate(eight_points(*values)):
            tw_re = twist_ref[0, k : k + 1, :]
            tw_im = twist_ref[1, k : k + 1, :]
            if k == 0:
                out_re, out_im = re, im
            else:
                out_re = re * tw_re - im * tw_im
                out_im = re * tw_im + im * tw_re
            row = (k * spans + g) * antennas
            part_ref[row : row + antennas, 0:second] = out_re.astype(jnp.bfloat16)
            part_ref[row : row + antennas, second:] = out_im.astype(jnp.bfloat16)
    copies[3].wait()
    both = jnp.concatenate([gain_ref[0], gain_ref[1]], axis=0)
    turn_ref[0:channels, 0 : 2 * antennas] = both.T
    copies[4].wait()
    blank = jnp.zeros(((2 * frames - spans) * antennas, second), jnp.float32)
    share = FIRST // PARTS
    lines = spans * antennas
    sends = []
    for h in range(PARTS):
        all_spectra = jnp.dot(
            part_ref[h * share * lines : (h + 1) * share * lines], table_ref[...],
            preferred_element_type=jnp.float32)
        for q in range(share):
            k = h * share + q
            spectra = all_spectra[q * lines : (q + 1) * lines]
            gains = turn_ref[pl.ds(k, second, stride=FIRST), 0 : 2 * antennas].T
            gain_re = jnp.concatenate([gains[0:antennas]] * spans, axis=0)
            gain_im = jnp.concatenate([gains[antennas:]] * spans, axis=0)
            re, im = spectra[:, 0:second], spectra[:, second:]
            for c, volts in enumerate((re * gain_re - im * gain_im, re * gain_im + im * gain_re)):
                turned = jnp.concatenate([volts, blank], axis=0).T
                sorted_ref[h, pl.ds(2 * q + c, second, stride=2 * share), :] = turned
        width = 2 * share
        pack_ref[:, h] = sorted_ref[h, 0 : second * width].reshape(second, width, second).astype(jnp.bfloat16)
        sends.append(pltpu.make_async_copy(pack_ref.at[:, h], out_ref.at[:, h], sems.at[len(copies) + h]))
        sends[-1].start()
    for send in sends:
        send.wait()


def footprint_kernel(cells_ref, offsets_ref, right_ref, left_ref):
    count = cells_ref.shape[1]
    rows, cols = cells_ref[0:1, :], cells_ref[1:2, :]
    share = (offsets_ref[...].astype(jnp.float32) + 0.5) * 0.125
    t_row, t_col = share[0:1, :], share[1:2, :]
    low = rows & (BAND - 1)
    place = (rows - low) * (GRID // BAND) + cols

    def table(height, first, weight):
        at = lax.broadcasted_iota(jnp.int32, (height, count), 0)
        near = jnp.where(at == first, 1.0 - weight, 0.0)
        return jnp.where(at == first + 1, weight, near).astype(jnp.bfloat16)

    right_ref[...] = table(BANDS * GRID, place, t_col)
    left_ref[...] = table(left_ref.shape[0], low, t_row)


def image_kernel(scale, x_ref, right_ref, left_ref, first_ref, second_ref, out_ref,
                 wide_ref, volt_ref, spread_ref, grid_ref, side_ref, sky_ref, sems):
    blocks = 4
    frames = 4
    antennas = 16
    step = 4 * blocks
    for d in range(128):
        wide_ref[d * IN_PITCH : d * IN_PITCH + step] = x_ref[d * step : (d + 1) * step].astype(jnp.float32)
    for kk in range(2):
        for c in range(2):
            tail = None
            for t in range(blocks):
                turned = wide_ref[pl.ds(4 * t + 2 * kk + c, 128, stride=IN_PITCH), :].T
                own = turned[0 : frames * antennas]
                if tail is not None:
                    own = jnp.concatenate(
                        [own[0 : (TAPS - 1) * antennas] + tail, own[(TAPS - 1) * antennas :]], axis=0)
                tail = turned[frames * antennas : (frames + TAPS - 1) * antennas]
                for f in range(frames):
                    row = (kk * blocks + t) * frames + f
                    volt_ref[row // CHUNK, 2 * (row % CHUNK) + c] = own[f * antennas : (f + 1) * antennas]

    members = 2 * CHUNK

    def chunk(i, carry):
        for a in range(antennas):
            lanes = slice(a * 128, (a + 1) * 128)
            left = left_ref[0:BAND, lanes]
            for m in range(members):
                row = volt_ref[i, m, a : a + 1, :].astype(jnp.bfloat16)
                spread_ref[m * BAND : (m + 1) * BAND, lanes] = left * row
            edge = volt_ref[i, :, a, :].astype(jnp.bfloat16)
            spread_ref[members * BAND :, lanes] = edge * left_ref[BAND : BAND + 1, lanes]
        grid_ref[...] = lax.dot_general(
            spread_ref[...], right_ref[...], (((1,), (1,)), ((), ())),
            preferred_element_type=jnp.float32)
        for m in range(members):
            grid_ref[m * BAND : m * BAND + 1, GRID:] += grid_ref[
                members * BAND + m : members * BAND + m + 1, : (BANDS - 1) * GRID]
        for f in range(CHUNK):
            for c in range(2):
                m = 2 * f + c
                for h in range(BANDS):
                    side_ref[i * CHUNK + f, h * BAND : (h + 1) * BAND, c * GRID : (c + 1) * GRID] = grid_ref[
                        m * BAND : (m + 1) * BAND, h * GRID : (h + 1) * GRID].astype(jnp.bfloat16)
        return carry

    lax.fori_loop(0, 2 * blocks * frames // CHUNK, chunk, 0)
    sends = []
    for kk in range(2):
        total = None
        for t in range(0, blocks * frames, GROUP):
            first = kk * blocks * frames + t
            side = side_ref[first : first + GROUP].reshape(GROUP * GRID, 2 * GRID)
            half = jnp.dot(side, first_ref[...], preferred_element_type=jnp.float32).astype(jnp.bfloat16)
            mid = jnp.concatenate([
                jnp.concatenate([
                    half[f * GRID : (f + 1) * GRID, c * GRID : (c + 1) * GRID] for f in range(GROUP)], axis=1)
                for c in range(2)], axis=0)
            sky = jnp.dot(second_ref[...], mid, preferred_element_type=jnp.float32)
            power = sky[0:GRID] * sky[0:GRID] + sky[GRID:] * sky[GRID:]
            for f in range(GROUP):
                part = power[:, f * GRID : (f + 1) * GRID]
                total = part if total is None else total + part
        sky_ref[kk] = total * scale
        sends.append(pltpu.make_async_copy(sky_ref.at[kk], out_ref.at[kk], sems.at[kk]))
        sends[-1].start()
    for send in sends:
        send.wait()


def local(voltages, calibrated_gain, cells, offsets):
    _, frames, antennas, channels = voltages.shape
    second = channels // FIRST
    devices = lax.axis_size("chan") * lax.axis_size("tblk")
    all_antennas = antennas * lax.axis_size("chan")
    scale = 1.0 / (all_antennas * channels * frames * lax.axis_size("tblk"))
    rows = channels * 2

    send = pl.pallas_call(
        lambda *refs: channelize_kernel(frames, *refs),
        out_shape=jax.ShapeDtypeStruct((second, PARTS, rows // second // PARTS, second), jnp.bfloat16),
        out_specs=pl.BlockSpec(memory_space=pl.ANY),
        in_specs=[pl.BlockSpec(memory_space=pl.ANY)] * 5,
        scratch_shapes=[
            pltpu.VMEM(voltages.shape, jnp.bfloat16),
            pltpu.VMEM(calibrated_gain.shape, jnp.float32),
            pltpu.VMEM((TAPS, channels), jnp.float32),
            pltpu.VMEM((2, FIRST, second), jnp.float32),
            pltpu.VMEM((2 * second, 2 * second), jnp.bfloat16),
            pltpu.VMEM((FIRST * (frames + TAPS - 1) * antennas, 2 * second), jnp.bfloat16),
            pltpu.VMEM((channels + FIRST, 128), jnp.float32),
            pltpu.VMEM((PARTS, rows // PARTS + FIRST, second), jnp.float32),
            pltpu.VMEM((second, PARTS, rows // second // PARTS, second), jnp.bfloat16),
            pltpu.SemaphoreType.DMA((5 + PARTS,)),
        ],
        compiler_params=pltpu.CompilerParams(vmem_limit_bytes=60 * 1024 * 1024),
        name="channelize",
    )(
        voltages, calibrated_gain, jnp.asarray(prototype(channels)),
        jnp.asarray(twiddle(channels)), jnp.asarray(dft_right(second)),
    )

    def by_member(table):
        return table.reshape(2, all_antennas // antennas, antennas).transpose(0, 2, 1).reshape(2, all_antennas)

    right, left = pl.pallas_call(
        footprint_kernel,
        out_shape=(
            jax.ShapeDtypeStruct((BANDS * GRID, all_antennas), jnp.bfloat16),
            jax.ShapeDtypeStruct((BAND + 16, all_antennas), jnp.bfloat16),
        ),
        compiler_params=pltpu.CompilerParams(vmem_limit_bytes=VMEM_BYTES),
        cost_estimate=pl.CostEstimate(flops=10_000_000, bytes_accessed=1_500_000, transcendentals=0),
        name="footprint",
    )(by_member(cells), by_member(offsets))

    send = send.reshape(devices, rows // devices, second)
    received = lax.all_to_all(send, ("chan", "tblk"), split_axis=0, concat_axis=0, tiled=True)
    received = received.reshape(rows, second)

    members = 2 * CHUNK
    chunks = 2 * frames * lax.axis_size("tblk") // CHUNK
    return pl.pallas_call(
        lambda *refs: image_kernel(scale, *refs),
        out_shape=jax.ShapeDtypeStruct((2, GRID, GRID), jnp.float32),
        out_specs=pl.BlockSpec(memory_space=pl.ANY),
        scratch_shapes=[
            pltpu.VMEM((128 * IN_PITCH + 16, second), jnp.float32),
            pltpu.VMEM((chunks, members, antennas, 128), jnp.float32),
            pltpu.VMEM((members * (BAND + 1), all_antennas), jnp.bfloat16),
            pltpu.VMEM((members * (BAND + 1), BANDS * GRID), jnp.float32),
            pltpu.VMEM((chunks * CHUNK, GRID, 2 * GRID), jnp.bfloat16),
            pltpu.VMEM((2, GRID, GRID), jnp.float32),
            pltpu.SemaphoreType.DMA((2,)),
        ],
        compiler_params=pltpu.CompilerParams(vmem_limit_bytes=VMEM_BYTES),
        name="image",
    )(received, right, left, jnp.asarray(dft_right(GRID)), jnp.asarray(dft_left(GRID)))


def solution(mesh):
    placed = (P(None, "tblk", "chan", None), P(None, "chan", None), P(), P())
    return jax.shard_map(
        local,
        mesh=mesh,
        in_specs=placed,
        out_specs=P(("chan", "tblk"), None, None),
        check_vma=False,
    )
```

```python
import math

import jax
import jax.numpy as jnp
import numpy as np
from jax import lax
from jax.experimental import pallas as pl
from jax.experimental.pallas import tpu as pltpu
from jax.sharding import PartitionSpec as P

GRID = 128
TAPS = 4
FIRST = 8
BANDS = 4
BAND = GRID // BANDS
PARTS = 2
IN_PITCH = 17
GROUP = 4
CHUNK = 16
VMEM_BYTES = 32 * 1024 * 1024


def prototype(channels):
    span = TAPS * channels
    places = np.arange(span, dtype=np.float64) + 0.5
    window = 0.54 - 0.46 * np.cos(places * (2.0 * math.pi / span))
    return (np.sinc((places - 0.5 * span) / channels) * window).reshape(TAPS, channels).astype(np.float32)


def twiddle(channels):
    second = channels // FIRST
    phases = (np.arange(FIRST)[:, None] * np.arange(second)[None, :] % channels) * (2.0 * math.pi / channels)
    return np.stack([np.cos(phases), -np.sin(phases)]).astype(np.float32)


def dft_parts(length):
    points = np.arange(length)
    phases = (points[:, None] * points[None, :] % length) * (2.0 * math.pi / length)
    return np.cos(phases), np.sin(phases)


def dft_right(length):
    cosine, sine = dft_parts(length)
    return np.block([[cosine, -sine], [sine, cosine]]).astype(jnp.bfloat16)


def dft_left(length):
    cosine, sine = dft_parts(length)
    return np.block([[cosine, sine], [-sine, cosine]]).astype(jnp.bfloat16)


def eight_points(re, im):
    add = lambda p, q: (p[0] + q[0], p[1] + q[1])
    sub = lambda p, q: (p[0] - q[0], p[1] - q[1])
    sub_i = lambda p, q: (p[0] + q[1], p[1] - q[0])
    add_i = lambda p, q: (p[0] - q[1], p[1] + q[0])
    root = math.sqrt(0.5)
    w = list(zip(re, im))
    a0, a1, a2, a3 = add(w[0], w[4]), sub(w[0], w[4]), add(w[2], w[6]), sub(w[2], w[6])
    a4, a5, a6, a7 = add(w[1], w[5]), sub(w[1], w[5]), add(w[3], w[7]), sub(w[3], w[7])
    b0, b2, b1, b3 = add(a0, a2), sub(a0, a2), sub_i(a1, a3), add_i(a1, a3)
    b4, b6, b5, b7 = add(a4, a6), sub(a4, a6), sub_i(a5, a7), add_i(a5, a7)
    c5 = ((b5[0] + b5[1]) * root, (b5[1] - b5[0]) * root)
    c7 = ((b7[1] - b7[0]) * root, (b7[0] + b7[1]) * -root)
    return [
        add(b0, b4), add(b1, c5), sub_i(b2, b6), add(b3, c7),
        sub(b0, b4), sub(b1, c5), add_i(b2, b6), sub(b3, c7),
    ]


def channelize_kernel(frames, volt_hbm, gain_hbm, taps_hbm, twist_hbm, table_hbm, out_ref,
                      volt_ref, gain_ref, taps_ref, twist_ref, table_ref,
                      part_ref, turn_ref, sorted_ref, pack_ref, sems):
    sources = (volt_hbm, taps_hbm, twist_hbm, gain_hbm, table_hbm)
    targets = (volt_ref, taps_ref, twist_ref, gain_ref, table_ref)
    copies = [pltpu.make_async_copy(s, t, sems.at[i]) for i, (s, t) in enumerate(zip(sources, targets))]
    for copy in copies:
        copy.start()
    antennas = volt_ref.shape[2]
    channels = volt_ref.shape[3]
    second = channels // FIRST
    spans = frames + TAPS - 1
    for copy in copies[0:3]:
        copy.wait()
    for g in range(spans):
        values = []
        for c in range(2):
            total = None
            for p in range(TAPS):
                f = g - (TAPS - 1) + p
                if 0 <= f < frames:
                    term = volt_ref[c, f].astype(jnp.float32) * taps_ref[p : p + 1, :]
                    total = term if total is None else total + term
            total = total.astype(jnp.bfloat16).astype(jnp.float32)
            values.append([total[:, j * second : (j + 1) * second] for j in range(FIRST)])
        for k, (re, im) in enumerate(eight_points(*values)):
            tw_re = twist_ref[0, k : k + 1, :]
            tw_im = twist_ref[1, k : k + 1, :]
            if k == 0:
                out_re, out_im = re, im
            else:
                out_re = re * tw_re - im * tw_im
                out_im = re * tw_im + im * tw_re
            row = (k * spans + g) * antennas
            part_ref[row : row + antennas, 0:second] = out_re.astype(jnp.bfloat16)
            part_ref[row : row + antennas, second:] = out_im.astype(jnp.bfloat16)
    copies[3].wait()
    both = jnp.concatenate([gain_ref[0], gain_ref[1]], axis=0)
    turn_ref[0:channels, 0 : 2 * antennas] = both.T
    copies[4].wait()
    blank = jnp.zeros(((2 * frames - spans) * antennas, second), jnp.float32)
    share = FIRST // PARTS
    lines = spans * antennas
    sends = []
    for h in range(PARTS):
        all_spectra = jnp.dot(
            part_ref[h * share * lines : (h + 1) * share * lines], table_ref[...],
            preferred_element_type=jnp.float32)
        for q in range(share):
            k = h * share + q
            spectra = all_spectra[q * lines : (q + 1) * lines]
            gains = turn_ref[pl.ds(k, second, stride=FIRST), 0 : 2 * antennas].T
            gain_re = jnp.concatenate([gains[0:antennas]] * spans, axis=0)
            gain_im = jnp.concatenate([gains[antennas:]] * spans, axis=0)
            re, im = spectra[:, 0:second], spectra[:, second:]
            for c, volts in enumerate((re * gain_re - im * gain_im, re * gain_im + im * gain_re)):
                turned = jnp.concatenate([volts, blank], axis=0).T
                sorted_ref[h, pl.ds(2 * q + c, second, stride=2 * share), :] = turned
        width = 2 * share
        pack_ref[:, h] = sorted_ref[h, 0 : second * width].reshape(second, width, second).astype(jnp.bfloat16)
        sends.append(pltpu.make_async_copy(pack_ref.at[:, h], out_ref.at[:, h], sems.at[len(copies) + h]))
        sends[-1].start()
    for send in sends:
        send.wait()


def footprint_kernel(cells_ref, offsets_ref, right_ref, left_ref):
    count = cells_ref.shape[1]
    rows, cols = cells_ref[0:1, :], cells_ref[1:2, :]
    share = (offsets_ref[...].astype(jnp.float32) + 0.5) * 0.125
    t_row, t_col = share[0:1, :], share[1:2, :]
    low = rows & (BAND - 1)
    place = (rows - low) * (GRID // BAND) + cols

    def table(height, first, weight):
        at = lax.broadcasted_iota(jnp.int32, (height, count), 0)
        near = jnp.where(at == first, 1.0 - weight, 0.0)
        return jnp.where(at == first + 1, weight, near).astype(jnp.bfloat16)

    right_ref[...] = table(BANDS * GRID, place, t_col)
    left_ref[...] = table(left_ref.shape[0], low, t_row)


def image_kernel(scale, x_ref, right_ref, left_ref, first_ref, second_ref, out_ref,
                 wide_ref, volt_ref, spread_ref, grid_ref, side_ref):
    blocks = 4
    frames = 4
    antennas = 16
    step = 4 * blocks
    for d in range(128):
        wide_ref[d * IN_PITCH : d * IN_PITCH + step] = x_ref[d * step : (d + 1) * step].astype(jnp.float32)
    for kk in range(2):
        for c in range(2):
            tail = None
            for t in range(blocks):
                turned = wide_ref[pl.ds(4 * t + 2 * kk + c, 128, stride=IN_PITCH), :].T
                own = turned[0 : frames * antennas]
                if tail is not None:
                    own = jnp.concatenate(
                        [own[0 : (TAPS - 1) * antennas] + tail, own[(TAPS - 1) * antennas :]], axis=0)
                tail = turned[frames * antennas : (frames + TAPS - 1) * antennas]
                for f in range(frames):
                    row = (kk * blocks + t) * frames + f
                    volt_ref[row // CHUNK, 2 * (row % CHUNK) + c] = own[f * antennas : (f + 1) * antennas]

    members = 2 * CHUNK

    def chunk(i, carry):
        for a in range(antennas):
            lanes = slice(a * 128, (a + 1) * 128)
            left = left_ref[0:BAND, lanes]
            for m in range(members):
                row = volt_ref[i, m, a : a + 1, :].astype(jnp.bfloat16)
                spread_ref[m * BAND : (m + 1) * BAND, lanes] = left * row
            edge = volt_ref[i, :, a, :].astype(jnp.bfloat16)
            spread_ref[members * BAND :, lanes] = edge * left_ref[BAND : BAND + 1, lanes]
        grid_ref[...] = lax.dot_general(
            spread_ref[...], right_ref[...], (((1,), (1,)), ((), ())),
            preferred_element_type=jnp.float32)
        for m in range(members):
            grid_ref[m * BAND : m * BAND + 1, GRID:] += grid_ref[
                members * BAND + m : members * BAND + m + 1, : (BANDS - 1) * GRID]
        for f in range(CHUNK):
            for c in range(2):
                m = 2 * f + c
                for h in range(BANDS):
                    side_ref[i * CHUNK + f, h * BAND : (h + 1) * BAND, c * GRID : (c + 1) * GRID] = grid_ref[
                        m * BAND : (m + 1) * BAND, h * GRID : (h + 1) * GRID].astype(jnp.bfloat16)
        return carry

    lax.fori_loop(0, 2 * blocks * frames // CHUNK, chunk, 0)
    for kk in range(2):
        total = None
        for t in range(0, blocks * frames, GROUP):
            first = kk * blocks * frames + t
            side = side_ref[first : first + GROUP].reshape(GROUP * GRID, 2 * GRID)
            half = jnp.dot(side, first_ref[...], preferred_element_type=jnp.float32).astype(jnp.bfloat16)
            mid = jnp.concatenate([
                jnp.concatenate([
                    half[f * GRID : (f + 1) * GRID, c * GRID : (c + 1) * GRID] for f in range(GROUP)], axis=1)
                for c in range(2)], axis=0)
            sky = jnp.dot(second_ref[...], mid, preferred_element_type=jnp.float32)
            power = sky[0:GRID] * sky[0:GRID] + sky[GRID:] * sky[GRID:]
            for f in range(GROUP):
                part = power[:, f * GRID : (f + 1) * GRID]
                total = part if total is None else total + part
        out_ref[kk] = total * scale


def local(voltages, calibrated_gain, cells, offsets):
    _, frames, antennas, channels = voltages.shape
    second = channels // FIRST
    devices = lax.axis_size("chan") * lax.axis_size("tblk")
    all_antennas = antennas * lax.axis_size("chan")
    scale = 1.0 / (all_antennas * channels * frames * lax.axis_size("tblk"))
    rows = channels * 2

    send = pl.pallas_call(
        lambda *refs: channelize_kernel(frames, *refs),
        out_shape=jax.ShapeDtypeStruct((second, PARTS, rows // second // PARTS, second), jnp.bfloat16),
        out_specs=pl.BlockSpec(memory_space=pl.ANY),
        in_specs=[pl.BlockSpec(memory_space=pl.ANY)] * 5,
        scratch_shapes=[
            pltpu.VMEM(voltages.shape, jnp.bfloat16),
            pltpu.VMEM(calibrated_gain.shape, jnp.float32),
            pltpu.VMEM((TAPS, channels), jnp.float32),
            pltpu.VMEM((2, FIRST, second), jnp.float32),
            pltpu.VMEM((2 * second, 2 * second), jnp.bfloat16),
            pltpu.VMEM((FIRST * (frames + TAPS - 1) * antennas, 2 * second), jnp.bfloat16),
            pltpu.VMEM((channels + FIRST, 128), jnp.float32),
            pltpu.VMEM((PARTS, rows // PARTS + FIRST, second), jnp.float32),
            pltpu.VMEM((second, PARTS, rows // second // PARTS, second), jnp.bfloat16),
            pltpu.SemaphoreType.DMA((5 + PARTS,)),
        ],
        compiler_params=pltpu.CompilerParams(vmem_limit_bytes=60 * 1024 * 1024),
        name="channelize",
    )(
        voltages, calibrated_gain, jnp.asarray(prototype(channels)),
        jnp.asarray(twiddle(channels)), jnp.asarray(dft_right(second)),
    )

    def by_member(table):
        return table.reshape(2, all_antennas // antennas, antennas).transpose(0, 2, 1).reshape(2, all_antennas)

    right, left = pl.pallas_call(
        footprint_kernel,
        out_shape=(
            jax.ShapeDtypeStruct((BANDS * GRID, all_antennas), jnp.bfloat16),
            jax.ShapeDtypeStruct((BAND + 16, all_antennas), jnp.bfloat16),
        ),
        compiler_params=pltpu.CompilerParams(vmem_limit_bytes=VMEM_BYTES),
        cost_estimate=pl.CostEstimate(flops=10_000_000, bytes_accessed=1_500_000, transcendentals=0),
        name="footprint",
    )(by_member(cells), by_member(offsets))

    send = send.reshape(devices, rows // devices, second)
    received = lax.all_to_all(send, ("chan", "tblk"), split_axis=0, concat_axis=0, tiled=True)
    received = received.reshape(rows, second)

    members = 2 * CHUNK
    chunks = 2 * frames * lax.axis_size("tblk") // CHUNK
    return pl.pallas_call(
        lambda *refs: image_kernel(scale, *refs),
        out_shape=jax.ShapeDtypeStruct((2, GRID, GRID), jnp.float32),
        scratch_shapes=[
            pltpu.VMEM((128 * IN_PITCH + 16, second), jnp.float32),
            pltpu.VMEM((chunks, members, antennas, 128), jnp.float32),
            pltpu.VMEM((members * (BAND + 1), all_antennas), jnp.bfloat16),
            pltpu.VMEM((members * (BAND + 1), BANDS * GRID), jnp.float32),
            pltpu.VMEM((chunks * CHUNK, GRID, 2 * GRID), jnp.bfloat16),
        ],
        compiler_params=pltpu.CompilerParams(vmem_limit_bytes=VMEM_BYTES),
        name="image",
    )(received, right, left, jnp.asarray(dft_right(GRID)), jnp.asarray(dft_left(GRID)))


def solution(mesh):
    placed = (P(None, "tblk", "chan", None), P(None, "chan", None), P(), P())
    return jax.shard_map(
        local,
        mesh=mesh,
        in_specs=placed,
        out_specs=P(("chan", "tblk"), None, None),
        check_vma=False,
    )
```
